32 devices in a mesh: phase: 2 (over x), lat: 2 (over core), lon: 8 (over z, y).
Axes of the slice: x: 2, y: 2, z: 4, core: 2. Of those that a mesh axis runs over, the one named last changes fastest.
Arguments:
- x_in: bfloat16 [2, 2, 12, 96, 512], P('phase', None, 'lat', 'lon'), may hold values from -430 to 430
- out_grad: bfloat16 [2, 2, 12, 96, 512], P('phase', None, 'lat', 'lon'), may hold values from -6 to 6
- w_qkv: bfloat16 [2, 1536, 512], P('phase'), may hold values from -0.25 to 0.25
- w_proj: bfloat16 [2, 512, 512], P('phase'), may hold values from -0.25 to 0.25
- norm_gain: float32 [2, 512], P('phase'), may hold values from 0.25 to 1.75
- bias_table: float32 [2, 8, 759], P('phase'), may hold values from -80 to 165
- lat_labels: int32 [12], P('lat'), may hold values from 0 to 2, never falling along the last dimension, each value on 1 to 8 neighbouring positions
Outputs:
- grad_input: bfloat16 [2, 2, 12, 96, 512], P('phase', None, 'lat', 'lon')
- grad_qkv: float32 [2, 1536, 512], P('phase', 'lat', 'lon')
The draws below stay inside these ranges and needn't reach their ends.
Inputs may be any that keep to these rules, and one draw needn't show every extreme that they name: `lat_labels`: labels never fall from one latitude row to the next; each label holds 1 to 8 consecutive rows, and one holds 8.
All inputs are finite; a program needn't handle non-finite values.
Results may differ from the reference program's by a relative error of at most 0.028.
Values may be sent and summed in bfloat16 or wider, within the bound.
A program may use at most 64 MiB of HBM per device.

```python
import math
import jax
import jax.numpy as jnp
import numpy as np
from jax import lax

D = 512
HEADS = 8
LEVELS = 2
WIN_LEV = 2
WIN_LAT = 6
WIN_LON = 12
NLAT = 12
NLON = 96
REL = 759


def draw_x_in(key, part):
    key = jax.random.fold_in(key, 11)
    subkeys = jax.random.split(key, 1)
    full_shape = (2, LEVELS, NLAT, NLON, D)
    base = jnp.clip(jax.random.normal(subkeys[0], full_shape, jnp.float32), -4.0, 4.0)
    return base.astype(jnp.bfloat16)


def draw_bias_table(key, part):
    key = jax.random.fold_in(key, 23)
    subkeys = jax.random.split(key, 1)
    full_shape = (2, HEADS, REL)
    return jnp.clip(jax.random.normal(subkeys[0], full_shape, jnp.float32), -4.0, 4.0)


def strengthened(result, stream_key, source, target, blocks, factor):
    owner, partner = [(jnp.arange(result.shape[dim]) // (result.shape[dim] // blocks)).reshape([-1 if axis == dim else 1 for axis in range(result.ndim)]) for dim in (source, target)]
    chosen = jax.random.permutation(stream_key, blocks)[partner]
    strong = (owner == chosen) | (owner == (partner + blocks // 2) % blocks)
    return jnp.where(strong, factor * result, result)


def shard_levels(rng, dims, shards, low, top_value):
    gain = 1.0
    for dim, blocks in shards:
        steps = jax.random.uniform(jax.random.fold_in(jax.random.fold_in(rng, 6), dim), (blocks,), jnp.float32, low / len(shards), top_value / len(shards))
        gain = gain * jnp.repeat(jnp.exp(steps), dims[dim] // blocks).reshape((-1,) + (1,) * (len(dims) - 1 - dim))
    return gain


def split_up(count, total, bound, lean):
    weights = [(1 << 20) // math.isqrt(grade ** lean) + 1 for grade in range(2, count + 1)]
    surplus, holding = total - bound - (count - 1), [1] * (count - 1)
    while surplus > 0:
        free = [i for i in range(count - 1) if holding[i] < bound]
        whole, left = sum([weights[i] for i in free]), surplus
        for i in free:
            addition = min(bound - holding[i], max(1, left * weights[i] // whole), surplus)
            holding[i] = holding[i] + addition
            surplus = surplus - addition
    return np.array([bound] + holding)


def uneven_parts(rng, count, total, limit, skew):
    if count == 2:
        one = jax.random.randint(rng, (), max(1, total - limit), min(limit, total - 1) + 1)
        return jnp.stack([one, total - one])
    lengths = jnp.asarray(split_up(count, total, limit, skew), jnp.int32)
    couples = (count - 1) // 2
    donor, taker = lengths[1:1 + 2 * couples:2], lengths[2:2 + 2 * couples:2]
    margin = jnp.minimum(donor - 1, limit - taker)
    passed = jax.random.randint(jax.random.fold_in(rng, 1), (couples,), 0, 1 << 20) % (margin + 1)
    lengths = lengths.at[1:1 + 2 * couples:2].set(donor - passed).at[2:2 + 2 * couples:2].set(taker + passed)
    return lengths[jax.random.permutation(jax.random.fold_in(rng, 2), count)]


def gaussian(rng, shape, deviation, bound, cuts=(), kind=jnp.bfloat16):
    array = jax.random.normal(rng, shape, jnp.float32) * deviation
    if len(cuts) > 0:
        array = shard_levels(rng, shape, cuts, -0.22, 0.18) * array
    return jnp.clip(array, min=-bound, max=bound).astype(kind)


def noise_with(own_key, dims, width, most, cuts, heavy, held_as=jnp.bfloat16):
    array = width * jax.random.normal(own_key, dims, jnp.float32)
    if cuts:
        array = array * shard_levels(own_key, dims, cuts, -0.22, 0.18)
    return jnp.clip(strengthened(array, jax.random.fold_in(own_key, 3), *heavy), -most, most).astype(held_as)


def setup_inputs(seed: int = 0) -> dict:
    splits = jax.random.split(jax.random.key(seed), 8)
    x_in = draw_x_in(jax.random.fold_in(splits[7], 71), 0)
    out_grad = noise_with(splits[1], (2, LEVELS, NLAT, NLON, D), 1.0, 6.0, ((0, 2), (2, 2), (3, 8)), (3, 4, 8, 2.0))
    w_qkv = gaussian(splits[2], (2, 3 * D, D), D ** -0.5, 0.25, ((0, 2),))
    w_proj = gaussian(splits[3], (2, D, D), D ** -0.5, 0.25, ((0, 2),))
    norm_gain = jnp.clip(1.0 + 0.15 * jax.random.normal(splits[4], (2, D), jnp.float32), 0.25, 1.75)
    bias_table = draw_bias_table(jax.random.fold_in(splits[7], 71), 0)
    lat_labels = jnp.searchsorted(jnp.cumsum(uneven_parts(splits[6], NLAT // 4, NLAT, 8, 0)), jnp.arange(NLAT), side="right").astype(jnp.int32)
    return dict(x_in=x_in, out_grad=out_grad, w_qkv=w_qkv, w_proj=w_proj, norm_gain=norm_gain, bias_table=bias_table, lat_labels=lat_labels)


EPSILON = 1e-05
MASKED = -1e+30

def mixing(formula, left_side, right_side):
    return jnp.einsum(formula, left_side.astype(jnp.float32), right_side.astype(jnp.float32))

def window_split(grid_field):
    levels, lat_rows, lon_cols, features = grid_field.shape
    grid_field = grid_field.reshape(levels // WIN_LEV, WIN_LEV, lat_rows // WIN_LAT, WIN_LAT, lon_cols // WIN_LON, WIN_LON, features)
    grid_field = grid_field.transpose(0, 2, 4, 1, 3, 5, 6)
    return grid_field.reshape(-1, WIN_LEV * WIN_LAT * WIN_LON, features)

def window_merge(blocks, levels, lat_rows, lon_cols):
    features = blocks.shape[-1]
    grid_field = blocks.reshape(levels // WIN_LEV, lat_rows // WIN_LAT, lon_cols // WIN_LON, WIN_LEV, WIN_LAT, WIN_LON, features)
    grid_field = grid_field.transpose(0, 3, 1, 4, 2, 5, 6)
    return grid_field.reshape(levels, lat_rows, lon_cols, features)

def make_tags(labels_shifted, levels, lon_cols):
    position = jnp.arange(levels, dtype=jnp.int32)
    region = jnp.where(position < levels - 2, 0, jnp.where(position == levels - 2, 1, 2)).astype(jnp.int32)
    tag_grid = 3 * labels_shifted[None, :, None] + region[:, None, None]
    tag_grid = jnp.broadcast_to(tag_grid, (levels, labels_shifted.shape[0], lon_cols))
    return window_split(tag_grid[..., None])[..., 0]

def selector(extent):
    offsets = jnp.arange(extent, dtype=jnp.int32)
    target = offsets[:, None] - offsets[None, :] + extent - 1
    return (target[:, :, None] == jnp.arange(2 * extent - 1, dtype=jnp.int32)[None, None, :]).astype(jnp.float32)

def window_bias(rel_table):
    head_count = rel_table.shape[0]
    table_grid = rel_table.reshape(head_count, 2 * WIN_LEV - 1, 2 * WIN_LAT - 1, 2 * WIN_LON - 1)
    highest = lax.Precision.HIGHEST
    step_one = jnp.einsum('habc,pqa->hpqbc', table_grid, selector(WIN_LEV), precision=highest)
    step_two = jnp.einsum('hpqbc,rsb->hpqrsc', step_one, selector(WIN_LAT), precision=highest)
    step_three = jnp.einsum('hpqrsc,tuc->hpqrstu', step_two, selector(WIN_LON), precision=highest)
    cell_count = WIN_LEV * WIN_LAT * WIN_LON
    return step_three.transpose(0, 1, 3, 5, 2, 4, 6).reshape(head_count, cell_count, cell_count)

def recompute(blocks, tag_blocks, qkv_weight, gain_vector, attn_bias):
    window_count, cell_count, features = blocks.shape
    head_dim = features // HEADS
    values_wide = blocks.astype(jnp.float32)
    center = lax.optimization_barrier(jnp.mean(values_wide, axis=-1, keepdims=True))
    spread = lax.optimization_barrier(jnp.mean(jnp.square(values_wide - center), axis=-1, keepdims=True))
    inv_std = lax.rsqrt(spread + EPSILON)
    normed = (values_wide - center) * inv_std
    scaled_input = (normed * gain_vector).astype(jnp.bfloat16)
    projected = mixing('wnd,ed->wne', scaled_input, qkv_weight).astype(jnp.bfloat16)
    split_heads = projected.reshape(window_count, cell_count, 3, HEADS, head_dim)
    query_heads = split_heads[:, :, 0]
    key_heads = split_heads[:, :, 1]
    value_heads = split_heads[:, :, 2]
    score_scale = head_dim ** (-0.5)
    scores = mixing('wihc,wjhc->whij', query_heads, key_heads) * score_scale + attn_bias[None]
    allowed = tag_blocks[:, None, :, None] == tag_blocks[:, None, None, :]
    scores = jnp.where(allowed, scores, MASKED)
    row_max = lax.optimization_barrier(jnp.max(scores, axis=-1, keepdims=True))
    weights = jnp.exp(scores - row_max)
    attention = weights / lax.optimization_barrier(jnp.sum(weights, axis=-1, keepdims=True))
    return (scaled_input, normed, inv_std, query_heads, key_heads, value_heads, attention, attention.astype(jnp.bfloat16))

def backprop(stored, grad_blocks, qkv_weight, proj_weight, gain_vector):
    scaled_input, normed, inv_std, query_heads, key_heads, value_heads, attention, attention_low = stored
    window_count, cell_count, features = grad_blocks.shape
    head_dim = features // HEADS
    score_scale = head_dim ** (-0.5)
    d_attended = mixing('wne,ed->wnd', grad_blocks, proj_weight).astype(jnp.bfloat16)
    d_heads = d_attended.reshape(window_count, cell_count, HEADS, head_dim)
    d_probs = mixing('wihc,wjhc->whij', d_heads, value_heads)
    d_value = mixing('whij,wihc->wjhc', attention_low, d_heads)
    inner_sum = lax.optimization_barrier(jnp.sum(attention * d_probs, axis=-1, keepdims=True))
    d_scores = (attention * (d_probs - inner_sum)).astype(jnp.bfloat16)
    d_query = mixing('whij,wjhc->wihc', d_scores, key_heads) * score_scale
    d_key = mixing('whij,wihc->wjhc', d_scores, query_heads) * score_scale
    d_qkv = jnp.stack([d_query, d_key, d_value], axis=2).reshape(window_count, cell_count, 3 * features)
    d_normed = mixing('wne,ed->wnd', d_qkv.astype(jnp.bfloat16), qkv_weight) * gain_vector
    d_shifted = inv_std * (d_normed - lax.optimization_barrier(jnp.mean(d_normed, axis=-1, keepdims=True)) - normed * lax.optimization_barrier(jnp.mean(d_normed * normed, axis=-1, keepdims=True)))
    return (d_shifted, d_qkv)

def phase_pass(blocks, tag_blocks, cotangents, qkv_weight, proj_weight, gain_vector, attn_bias, group_size):
    group_count = blocks.shape[0] // group_size
    features = blocks.shape[-1]

    def regroup(array_in):
        return array_in.reshape((group_count, group_size) + array_in.shape[1:])

    def one_group(running, pieces):
        stored = recompute(pieces[0], pieces[1], qkv_weight, gain_vector, attn_bias)
        results = [backprop(stored, member, qkv_weight, proj_weight, gain_vector) for member in pieces[2:]]
        summed = results[0][1]
        for further in results[1:]:
            summed = summed + further[1]
        grad_low = summed.astype(jnp.bfloat16).reshape(-1, 3 * features)
        flat_input = stored[0].reshape(-1, features)
        running = running + jnp.dot(grad_low.T, flat_input, preferred_element_type=jnp.float32)
        return (running, tuple((further[0] for further in results)))
    start_sum = jnp.zeros((3 * features, features), jnp.float32)
    pieces = (regroup(blocks), regroup(tag_blocks)) + tuple((regroup(member) for member in cotangents))
    running, outputs = lax.scan(one_group, start_sum, pieces)
    return (running, tuple((member.reshape(blocks.shape) for member in outputs)))

def reference(x_in, out_grad, w_qkv, w_proj, norm_gain, bias_table, lat_labels):
    lat_half = WIN_LAT // 2
    lon_half = WIN_LON // 2
    lev_half = WIN_LEV // 2

    def forward_roll(grid_field):
        return jnp.roll(grid_field, (-lev_half, -lat_half, -lon_half), axis=(0, 1, 2))

    def backward_roll(grid_field):
        return jnp.roll(grid_field, (lev_half, lat_half, lon_half), axis=(0, 1, 2))
    labels_shifted = jnp.roll(lat_labels, -lat_half)
    tag_blocks = make_tags(labels_shifted, LEVELS, NLON)
    group_size = NLON // WIN_LON

    def run_phase(phase_index, cotangents):
        blocks = window_split(forward_roll(x_in[phase_index]))
        cot_blocks = tuple((window_split(forward_roll(member)) for member in cotangents))
        attn_bias = window_bias(bias_table[phase_index])
        return phase_pass(blocks, tag_blocks, cot_blocks, w_qkv[phase_index], w_proj[phase_index], norm_gain[phase_index], attn_bias, group_size)
    total_dec, dec_parts = run_phase(1, (out_grad[1],))
    dec_grad = out_grad[1].astype(jnp.float32) + backward_roll(window_merge(dec_parts[0], LEVELS, NLAT, NLON))
    skip_grad = dec_grad.astype(jnp.bfloat16)
    total_enc, enc_parts = run_phase(0, (out_grad[0], skip_grad))
    first_part = out_grad[0].astype(jnp.float32) + backward_roll(window_merge(enc_parts[0], LEVELS, NLAT, NLON))
    second_part = skip_grad.astype(jnp.float32) + backward_roll(window_merge(enc_parts[1], LEVELS, NLAT, NLON))
    enc_grad = first_part + second_part
    grad_input = jnp.stack([enc_grad.astype(jnp.bfloat16), skip_grad])
    grad_qkv = jnp.stack([total_enc, total_dec])
    return (grad_input, grad_qkv)
```

```python
import functools

import jax
import jax.numpy as jnp
import ml_dtypes
import numpy as np
from jax import lax
from jax.experimental import pallas as pl
from jax.experimental.pallas import tpu as pltpu
from jax.sharding import PartitionSpec as P

HEADS = 8
EPSILON = 1e-05
MASKED = -1e30
MESH = pl.DeviceIdType.MESH
BF = jnp.bfloat16
F32 = jnp.float32

LEV, LAT, LON = 2, 6, 12
CELLS = LAT * LON
ROWS = 80
WROWS = LEV * ROWS
QROWS = 48
XROWS = LEV * LAT * 16


def permutations():
    to_quadrant = np.zeros((4 * QROWS, XROWS), np.float32)
    to_window = np.zeros((WROWS, 4 * QROWS), np.float32)
    for p in range(LEV):
        for i in range(LAT):
            for j in range(LON):
                ih, ii = divmod(i, LAT // 2)
                jh, jj = divmod(j, LON // 2)
                quad = QROWS * (2 * ih + jh) + 18 * p + 6 * ii + jj
                to_quadrant[quad, 16 * (LAT * p + i) + j] = 1
                row = ROWS * (1 - p) + LON * (ii + 3 * (1 - ih)) + jj + 6 * (1 - jh)
                to_window[row, quad] = 1
    column = np.zeros((128, 128), np.float32)
    label_row = np.zeros((128, 128), np.float32)
    for n in range(CELLS):
        i, j = divmod(n, LON)
        column[126 - (23 * i + j), n] = 1
        label_row[(i + 3) % 6, n] = 1
    return [
        m.astype(ml_dtypes.bfloat16)
        for m in (to_quadrant, to_window, to_window.T, to_quadrant.T, column, label_row)
    ]


def dot(a, b, dims=((1,), (0,))):
    return lax.dot_general(a, b, (dims, ((), ())), preferred_element_type=F32)


NT = ((1,), (1,))
TN = ((0,), (0,))


def kernel(
    n_lat, n_lon, chunk,
    x_ref, og_ref, wqkv_ref, wproj_ref, gain_ref, table_ref, labels_ref,
    to_quad_ref, to_win_ref, from_win_ref, from_quad_ref, column_ref, label_row_ref,
    gin_ref, gq_ref,
    pad_x, pad_og, send_q, recv_q, send_lab, recv_lab, rolled, expanded, bias,
    proj, att, dqkv, cot, skip, back_send, back_recv,
    scaled, scaled_in, low, low_in, part, part_in, summed, summed_in,
    halo_s, halo_r, lab_s, lab_r, skip_s, skip_r, back_s, back_r,
    sc_s, sc_r, low_s, low_r, pair_s, pair_r, grp_s, grp_r,
):
    ph, la, lo = lax.axis_index("phase"), lax.axis_index("lat"), lax.axis_index("lon")
    features = x_ref.shape[-1]
    cols = gq_ref.shape[0]
    rows = gq_ref.shape[1]
    half = n_lon // 2
    chunks = cols // chunk
    par = lax.rem(lo, 2)
    grp = lo // 2

    def device(dlat, dlon):
        return (ph, lax.rem(la + dlat + n_lat, n_lat), lax.rem(lo + dlon + n_lon, n_lon))

    offsets = set()
    for dlat, dlon in ((0, 1), (1, 0), (1, 1)):
        offsets |= {(dlat % n_lat, dlon % n_lon), (-dlat % n_lat, -dlon % n_lon)}
    offsets |= {(d, 0) for d in range(1, n_lat)}
    offsets |= {(0, 2 * d) for d in range(1, half)}
    offsets = sorted(offsets)
    barrier = pltpu.get_barrier_semaphore()
    for dlat, dlon in offsets:
        pl.semaphore_signal(barrier, inc=1, device_id=device(dlat, dlon), device_id_type=MESH)
    pl.semaphore_signal(barrier, inc=1, device_id=(1 - ph, la, lo), device_id_type=MESH)

    pad_x[...] = jnp.zeros_like(pad_x)
    pad_og[...] = jnp.zeros_like(pad_og)
    for k in range(LEV * LAT):
        pad_x[16 * k:16 * k + LON, :] = x_ref[k]
        pad_og[16 * k:16 * k + LON, :] = og_ref[k]
    quad_x = dot(to_quad_ref[...], pad_x[...]).astype(BF)
    quad_og = dot(to_quad_ref[...], pad_og[...]).astype(BF)
    for q in range(4):
        send_q[q, 0] = quad_x[QROWS * q:QROWS * (q + 1)]
        send_q[q, 1] = quad_og[QROWS * q:QROWS * (q + 1)]
    lane = lax.broadcasted_iota(jnp.int32, (8, 128), 1)
    own_lab = jnp.zeros((8, 128), F32)
    for i in range(LAT):
        own_lab = jnp.where(lane == i, labels_ref[i].astype(F32), own_lab)
    send_lab[...] = own_lab

    pl.semaphore_wait(barrier, len(offsets) + 1)

    halo = []
    for q, (dlat, dlon) in enumerate(((-1, -1), (-1, 0), (0, -1))):
        halo.append(pltpu.make_async_remote_copy(
            send_q.at[q], recv_q.at[q], halo_s.at[q], halo_r.at[q],
            device_id=device(dlat, dlon), device_id_type=MESH))
        halo[-1].start()
    lab_copy = pltpu.make_async_remote_copy(
        send_lab, recv_lab, lab_s.at[0], lab_r.at[0],
        device_id=device(-1, 0), device_id_type=MESH)
    lab_copy.start()
    recv_q[3] = send_q[3]

    table = table_ref[:, 128:512]
    for m in range(CELLS):
        i, j = divmod(m, LON)
        shift = (384 - (125 + 23 * i + j)) % 384
        rolled[8 * m:8 * m + 8, :] = pltpu.roll(table, shift, 1)[:, :128]
    wide = rolled[...]
    high = wide.astype(BF)
    rest = wide - high.astype(F32)
    mid = rest.astype(BF)
    least = (rest - mid.astype(F32)).astype(BF)
    column = column_ref[...]
    expanded[...] = (dot(high, column) + dot(mid, column)) + dot(least, column)

    lab_copy.wait()
    lab = jnp.where(lane < 3, recv_lab[...], own_lab)
    lab_row = dot(jnp.concatenate([lab, lab], axis=0).astype(BF), label_row_ref[...])[0:1]
    lane1 = lax.broadcasted_iota(jnp.int32, (1, 128), 1)
    lab_row = jnp.where(lane1 < CELLS, lab_row, -1.0)
    row_id = lax.broadcasted_iota(jnp.int32, (ROWS, 128), 0)
    lane_id = lax.broadcasted_iota(jnp.int32, (ROWS, 128), 1)
    want = jnp.zeros((ROWS, 128), jnp.int32)
    for i in range(LAT):
        want = jnp.where(row_id >= LON * i, (i + 3) % 6, want)
    lab_col = jnp.sum(jnp.where(lane_id == want, lab[0:1], 0.0), axis=1, keepdims=True)
    row1 = lax.broadcasted_iota(jnp.int32, (ROWS, 1), 0)
    lab_col = jnp.where(row1 < CELLS, lab_col, -1.0)
    allowed = lab_col == lab_row
    for h in range(HEADS):
        one = expanded[pl.ds(h, CELLS, stride=8), :]
        one = jnp.concatenate([one, jnp.zeros((ROWS - CELLS, 128), F32)], axis=0)
        bias[h // 2, ROWS * (h % 2):ROWS * (h % 2 + 1), :] = jnp.where(allowed, one, MASKED)

    for copy in halo:
        copy.wait()
    to_win = to_win_ref[...]
    x = dot(to_win, jnp.concatenate([recv_q[q, 0] for q in range(4)], axis=0))
    og = dot(to_win, jnp.concatenate([recv_q[q, 1] for q in range(4)], axis=0))
    gain = gain_ref[...]
    center = jnp.mean(x, axis=-1, keepdims=True)
    spread = jnp.mean(jnp.square(x - center), axis=-1, keepdims=True)
    inv_std = lax.rsqrt(spread + EPSILON)
    normed = (x - center) * inv_std
    scaled[...] = (normed * gain).astype(BF)
    sc_copies = []
    for d in range(1, n_lat):
        sc_copies.append(pltpu.make_async_remote_copy(
            scaled, scaled_in.at[d - 1], sc_s.at[d - 1], sc_r.at[d - 1],
            device_id=device(d, 0), device_id_type=MESH))
        sc_copies[-1].start()
    proj[...] = dot(scaled[...], wqkv_ref[...], NT).astype(BF)
    first_half = lax.broadcasted_iota(jnp.int32, (ROWS, 128), 1) < 64
    zero = jnp.zeros((ROWS, 128), BF)

    def both(pair):
        return jnp.concatenate(
            [jnp.where(first_half, pair, zero), jnp.where(first_half, zero, pair)], axis=0)

    def query_pair(p, hp):
        pair = proj[ROWS * p:ROWS * (p + 1), 128 * hp:128 * (hp + 1)]
        return both(pair * jnp.asarray(0.125, BF))

    def later_pair(which, p, hp):
        start = features * which + 128 * hp
        return proj[ROWS * p:ROWS * (p + 1), start:start + 128]

    for p in range(LEV):
        for hp in range(HEADS // 2):
            scores = dot(query_pair(p, hp), later_pair(1, p, hp), NT) + bias[hp][:, :ROWS]
            weights = jnp.exp(scores - jnp.max(scores, axis=-1, keepdims=True))
            att[4 * p + hp] = weights / jnp.sum(weights, axis=-1, keepdims=True)

    def backprop(cotangent, accumulate):
        d_attended = dot(cotangent, wproj_ref[...]).astype(BF)
        lows = []
        for p in range(LEV):
            parts = [[], [], []]
            for hp in range(HEADS // 2):
                d_pair = both(d_attended[ROWS * p:ROWS * (p + 1), 128 * hp:128 * (hp + 1)])
                attention = att[4 * p + hp]
                d_probs = dot(d_pair, later_pair(2, p, hp), NT)
                d_value = dot(attention.astype(BF), d_pair, TN)
                inner = jnp.sum(attention * d_probs, axis=-1, keepdims=True)
                d_scores = (attention * (d_probs - inner)).astype(BF)
                d_both = dot(d_scores, later_pair(1, p, hp))
                d_query = jnp.where(first_half, d_both[:ROWS], d_both[ROWS:]) * 0.125
                d_key = dot(d_scores, query_pair(p, hp), TN)
                for which, value in enumerate((d_query, d_key, d_value)):
                    start = features * which + 128 * hp
                    parts[which].append(value.astype(BF))
                    at = (slice(ROWS * p, ROWS * (p + 1)), slice(start, start + 128))
                    dqkv[at] = dqkv[at] + value if accumulate else value
            lows.append(jnp.concatenate(parts[0] + parts[1] + parts[2], axis=1))
        d_low = jnp.concatenate(lows, axis=0)
        d_normed = dot(d_low, wqkv_ref[...]) * gain
        return inv_std * (
            d_normed
            - jnp.mean(d_normed, axis=-1, keepdims=True)
            - normed * jnp.mean(d_normed * normed, axis=-1, keepdims=True))

    total = og + backprop(og.astype(BF), False)
    cot[...] = total.astype(BF)
    skip_copy = pltpu.make_async_remote_copy(
        cot, skip, skip_s.at[0], skip_r.at[0],
        device_id=(1 - ph, la, lo), device_id_type=MESH)

    @pl.when(ph == 1)
    def _():
        skip_copy.start()
        skip_copy.wait_send()

    @pl.when(ph == 0)
    def _():
        skip_copy.wait_recv()
        received = skip[...]
        second = backprop(received, True)
        cot[...] = (total + (received.astype(F32) + second)).astype(BF)

    for l in range(n_lat):
        low[l] = dqkv[:, cols * l:cols * (l + 1)].astype(BF)
    low_copies = []
    for d in range(1, n_lat):
        to = device(d, 0)
        low_copies.append(pltpu.make_async_remote_copy(
            low.at[to[1]], low_in.at[d - 1], low_s.at[d - 1], low_r.at[d - 1],
            device_id=to, device_id_type=MESH))
        low_copies[-1].start()

    from_win = dot(from_win_ref[...], cot[...]).astype(BF)
    for q in range(4):
        back_send[q] = from_win[QROWS * q:QROWS * (q + 1)]
    back = []
    for q, (dlat, dlon) in enumerate(((1, 1), (1, 0), (0, 1))):
        back.append(pltpu.make_async_remote_copy(
            back_send.at[q], back_recv.at[q], back_s.at[q], back_r.at[q],
            device_id=device(dlat, dlon), device_id_type=MESH))
    back_recv[3] = back_send[3]

    for copy in sc_copies + low_copies:
        copy.wait()
    pair_to = (ph, la, lo + 1 - 2 * par)
    pairs = []
    for c in range(chunks):
        at = slice(chunk * c, chunk * (c + 1))
        value = dot(scaled[...], low[la][:, at], TN)
        for d in range(1, n_lat):
            value = value + dot(scaled_in[d - 1], low_in[d - 1][:, at], TN)
        value = value.astype(BF)
        for j in range(n_lon):
            part[c, j % 2, j // 2] = value[rows * j:rows * (j + 1)]
        pairs.append(pltpu.make_async_remote_copy(
            part.at[c, 1 - par], part_in.at[c], pair_s.at[c], pair_r.at[c],
            device_id=pair_to, device_id_type=MESH))
        pairs[-1].start()
    for copy in back:
        copy.start()
    groups = []
    for c in range(chunks):
        pairs[c].wait_recv()
        summed[c] = (part[c, par].astype(F32) + part_in[c].astype(F32)).astype(BF)
        for d in range(1, half):
            to = lax.rem(grp + d, half)
            groups.append(pltpu.make_async_remote_copy(
                summed.at[c, to], summed_in.at[c, d - 1],
                grp_s.at[c, d - 1], grp_r.at[c, d - 1],
                device_id=(ph, la, 2 * to + par), device_id_type=MESH))
            groups[-1].start()

    for copy in back:
        copy.wait()
    result = dot(
        from_quad_ref[...], jnp.concatenate([back_recv[q] for q in range(4)], axis=0)).astype(BF)
    for k in range(LEV * LAT):
        gin_ref[k] = result[16 * k:16 * k + LON]

    for copy in groups:
        copy.wait()
    for c in range(chunks):
        value = summed[c, grp].astype(F32)
        for d in range(1, half):
            value = value + summed_in[c, d - 1].astype(F32)
        gq_ref[chunk * c:chunk * (c + 1), :] = value.T
    for copy in pairs:
        copy.wait_send()


def per_device(n_lat, n_lon, x_in, out_grad, w_qkv, w_proj, norm_gain, bias_table, lat_labels):
    features = x_in.shape[-1]
    outs = w_qkv.shape[1]
    cols, rows = outs // n_lat, features // n_lon
    chunk = 256 if cols % 256 == 0 else cols
    chunks, half = cols // chunk, n_lon // 2
    vmem = pl.BlockSpec(memory_space=pltpu.VMEM)
    dma = lambda *shape: pltpu.SemaphoreType.DMA(shape)
    peers = max(n_lat - 1, 1)
    grid = (LEV * LAT, LON, features)
    constants = [jnp.asarray(m) for m in permutations()]
    grad_input, grad_qkv = pl.pallas_call(
        functools.partial(kernel, n_lat, n_lon, chunk),
        out_shape=(
            jax.ShapeDtypeStruct(grid, BF),
            jax.ShapeDtypeStruct((cols, rows), F32),
        ),
        in_specs=[vmem] * 6 + [pl.BlockSpec(memory_space=pltpu.SMEM)] + [vmem] * 6,
        out_specs=(vmem, vmem),
        scratch_shapes=[
            pltpu.VMEM((XROWS, features), BF),
            pltpu.VMEM((XROWS, features), BF),
            pltpu.VMEM((4, 2, QROWS, features), BF),
            pltpu.VMEM((4, 2, QROWS, features), BF),
            pltpu.VMEM((8, 128), F32),
            pltpu.VMEM((8, 128), F32),
            pltpu.VMEM((8 * CELLS, 128), F32),
            pltpu.VMEM((8 * CELLS, 128), F32),
            pltpu.VMEM((HEADS // 2, 2 * ROWS, 128), F32),
            pltpu.VMEM((WROWS, outs), BF),
            pltpu.VMEM((HEADS, 2 * ROWS, ROWS), F32),
            pltpu.VMEM((WROWS, outs), F32),
            pltpu.VMEM((WROWS, features), BF),
            pltpu.VMEM((WROWS, features), BF),
            pltpu.VMEM((4, QROWS, features), BF),
            pltpu.VMEM((4, QROWS, features), BF),
            pltpu.VMEM((WROWS, features), BF),
            pltpu.VMEM((peers, WROWS, features), BF),
            pltpu.VMEM((n_lat, WROWS, cols), BF),
            pltpu.VMEM((peers, WROWS, cols), BF),
            pltpu.VMEM((chunks, 2, half, rows, chunk), BF),
            pltpu.VMEM((chunks, half, rows, chunk), BF),
            pltpu.VMEM((chunks, half, rows, chunk), BF),
            pltpu.VMEM((chunks, half - 1, rows, chunk), BF),
            dma(3), dma(3), dma(1), dma(1), dma(1), dma(1), dma(3), dma(3),
            dma(peers), dma(peers), dma(peers), dma(peers),
            dma(chunks), dma(chunks), dma(chunks, half - 1), dma(chunks, half - 1),
        ],
        compiler_params=pltpu.CompilerParams(
            collective_id=0, has_side_effects=True, vmem_limit_bytes=48 * 1024 * 1024),
    )(
        x_in.reshape(grid), out_grad.reshape(grid), w_qkv[0], w_proj[0], norm_gain,
        bias_table[0], lat_labels, *constants)
    return grad_input.reshape(x_in.shape), grad_qkv[None]


def solution(mesh):
    in_specs = (
        P("phase", None, "lat", "lon", None),
        P("phase", None, "lat", "lon", None),
        P("phase", None, None),
        P("phase", None, None),
        P("phase", None),
        P("phase", None, None),
        P("lat"),
    )
    out_specs = (P("phase", None, "lat", "lon", None), P("phase", "lat", "lon"))
    return jax.shard_map(
        functools.partial(per_device, mesh.shape["lat"], mesh.shape["lon"]),
        mesh=mesh, in_specs=in_specs, out_specs=out_specs, check_vma=False)
```

```python
import functools

import jax
import jax.numpy as jnp
import numpy as np
from jax import lax
from jax.experimental import pallas as pl
from jax.experimental.pallas import tpu as pltpu
from jax.sharding import PartitionSpec as P

HEADS = 8
EPSILON = 1e-05
MASKED = -1e30
MESH = pl.DeviceIdType.MESH
BF = jnp.bfloat16
F32 = jnp.float32

LEV, LAT, LON = 2, 6, 12
CELLS = LAT * LON
ROWS = 80
WROWS = LEV * ROWS


def selections():
    packed = np.zeros((WROWS + 256, 256), np.float32)
    for n in range(CELLS):
        i, j = divmod(n, LON)
        for p in range(LEV):
            packed[ROWS * (1 - p) + n, LEV * n + p] = 1
        packed[WROWS + 126 - (23 * i + j), n] = 1
        packed[WROWS + 128 + (i + 3) % 6, n] = 1
    return packed


def dot(a, b, dims=((1,), (0,))):
    return lax.dot_general(a, b, (dims, ((), ())), preferred_element_type=F32)


NT = ((1,), (1,))
TN = ((0,), (0,))


def kernel(
    n_lat, n_lon, chunk,
    x_hbm, og_hbm, wqkv_hbm, wproj_hbm, gain_hbm, table_hbm, labels_hbm, select_hbm,
    gin_ref, gq_ref,
    win_x, win_og, wqkv_ref, wproj_ref, gain_ref, table_ref, labels_ref, select_ref,
    send_lab, recv_lab, rolled, expanded, bias, proj, att, dqkv, cot, skip, back_src,
    scaled, scaled_in, low, low_in, part, part_in, summed, summed_in,
    local_s, halo_s, halo_r, lab_s, lab_r, skip_s, skip_r, back_s, back_r,
    sc_s, sc_r, low_s, low_r, pair_s, pair_r, grp_s, grp_r,
):
    ph, la, lo = lax.axis_index("phase"), lax.axis_index("lat"), lax.axis_index("lon")
    features = gain_ref.shape[-1]
    rows, cols = gq_ref.shape
    half = n_lon // 2
    chunks = cols // chunk
    par = lax.rem(lo, 2)
    grp = lo // 2

    def device(dlat, dlon):
        return (ph, lax.rem(la + dlat + n_lat, n_lat), lax.rem(lo + dlon + n_lon, n_lon))

    offsets = set()
    for dlat, dlon in ((0, 1), (1, 0), (1, 1)):
        offsets |= {(dlat % n_lat, dlon % n_lon), (-dlat % n_lat, -dlon % n_lon)}
    offsets |= {(d, 0) for d in range(1, n_lat)}
    offsets |= {(0, 2 * d) for d in range(1, half)}
    offsets = sorted(offsets)
    barrier = pltpu.get_barrier_semaphore()
    for dlat, dlon in offsets:
        pl.semaphore_signal(barrier, inc=1, device_id=device(dlat, dlon), device_id_type=MESH)
    pl.semaphore_signal(barrier, inc=1, device_id=(1 - ph, la, lo), device_id_type=MESH)

    def quadrant(ref, ih, jh):
        return ref.at[pl.ds(ih * LAT // 2, LAT // 2), pl.ds(jh * LON // 2, LON // 2)]

    loads = []
    for k, (src, dst) in enumerate((
        (labels_hbm, labels_ref),
        (table_hbm, table_ref),
        (select_hbm, select_ref),
        (quadrant(x_hbm, 1, 1), quadrant(win_x, 0, 0)),
        (quadrant(og_hbm, 1, 1), quadrant(win_og, 0, 0)),
        (gain_hbm, gain_ref),
        (wqkv_hbm, wqkv_ref),
        (wproj_hbm, wproj_ref),
    )):
        loads.append(pltpu.make_async_copy(src, dst, local_s.at[k]))
        loads[-1].start()
    loads[0].wait()
    lane = lax.broadcasted_iota(jnp.int32, (8, 128), 1)
    own_lab = jnp.zeros((8, 128), F32)
    for i in range(LAT):
        own_lab = jnp.where(lane == i, labels_ref[i].astype(F32), own_lab)
    send_lab[...] = own_lab

    pl.semaphore_wait(barrier, len(offsets) + 1)

    halo = []
    for ih, jh in ((0, 0), (0, 1), (1, 0)):
        for src, dst in ((x_hbm, win_x), (og_hbm, win_og)):
            k = len(halo)
            halo.append(pltpu.make_async_remote_copy(
                quadrant(src, ih, jh), quadrant(dst, 1 - ih, 1 - jh), halo_s.at[k], halo_r.at[k],
                device_id=device(ih - 1, jh - 1), device_id_type=MESH))
            halo[-1].start()
    lab_copy = pltpu.make_async_remote_copy(
        send_lab, recv_lab, lab_s.at[0], lab_r.at[0],
        device_id=device(-1, 0), device_id_type=MESH)
    lab_copy.start()
    for copy in loads[1:3]:
        copy.wait()

    table = table_ref[:, 128:512]
    for m in range(CELLS):
        i, j = divmod(m, LON)
        shift = (384 - (125 + 23 * i + j)) % 384
        rolled[8 * m:8 * m + 8, :] = pltpu.roll(table, shift, 1)[:, :128]
    wide = rolled[...]
    high = wide.astype(BF)
    rest = wide - high.astype(F32)
    mid = rest.astype(BF)
    least = (rest - mid.astype(F32)).astype(BF)
    column = select_ref[WROWS:WROWS + 128, :128].astype(BF)
    expanded[...] = (dot(high, column) + dot(mid, column)) + dot(least, column)

    lab_copy.wait()
    lab = jnp.where(lane < 3, recv_lab[...], own_lab)
    lab_row = dot(jnp.concatenate([lab, lab], axis=0).astype(BF), select_ref[WROWS + 128:WROWS + 256, :128].astype(BF))[0:1]
    lane1 = lax.broadcasted_iota(jnp.int32, (1, 128), 1)
    lab_row = jnp.where(lane1 < CELLS, lab_row, -1.0)
    row_id = lax.broadcasted_iota(jnp.int32, (ROWS, 128), 0)
    lane_id = lax.broadcasted_iota(jnp.int32, (ROWS, 128), 1)
    want = jnp.zeros((ROWS, 128), jnp.int32)
    for i in range(LAT):
        want = jnp.where(row_id >= LON * i, (i + 3) % 6, want)
    lab_col = jnp.sum(jnp.where(lane_id == want, lab[0:1], 0.0), axis=1, keepdims=True)
    row1 = lax.broadcasted_iota(jnp.int32, (ROWS, 1), 0)
    lab_col = jnp.where(row1 < CELLS, lab_col, -1.0)
    allowed = lab_col == lab_row
    for h in range(HEADS):
        one = expanded[pl.ds(h, CELLS, stride=8), :]
        one = jnp.concatenate([one, jnp.zeros((ROWS - CELLS, 128), F32)], axis=0)
        bias[h // 2, ROWS * (h % 2):ROWS * (h % 2 + 1), :] = jnp.where(allowed, one, MASKED)

    for copy in loads[3:] + halo:
        copy.wait()
    to_win = select_ref[:WROWS, :LEV * CELLS].astype(BF)
    x = dot(to_win, win_x[...].reshape(LEV * CELLS, features))
    og = dot(to_win, win_og[...].reshape(LEV * CELLS, features))
    gain = gain_ref[...]
    center = jnp.mean(x, axis=-1, keepdims=True)
    spread = jnp.mean(jnp.square(x - center), axis=-1, keepdims=True)
    inv_std = lax.rsqrt(spread + EPSILON)
    normed = (x - center) * inv_std
    scaled[...] = (normed * gain).astype(BF)
    sc_copies = []
    for d in range(1, n_lat):
        sc_copies.append(pltpu.make_async_remote_copy(
            scaled, scaled_in.at[d - 1], sc_s.at[d - 1], sc_r.at[d - 1],
            device_id=device(d, 0), device_id_type=MESH))
        sc_copies[-1].start()
    proj[...] = dot(scaled[...], wqkv_ref[...], NT).astype(BF)
    first_half = lax.broadcasted_iota(jnp.int32, (ROWS, 128), 1) < 64
    zero = jnp.zeros((ROWS, 128), BF)

    def both(pair):
        return jnp.concatenate(
            [jnp.where(first_half, pair, zero), jnp.where(first_half, zero, pair)], axis=0)

    def query_pair(p, hp):
        pair = proj[ROWS * p:ROWS * (p + 1), 128 * hp:128 * (hp + 1)]
        return both(pair * jnp.asarray(0.125, BF))

    def later_pair(which, p, hp):
        start = features * which + 128 * hp
        return proj[ROWS * p:ROWS * (p + 1), start:start + 128]

    for p in range(LEV):
        for hp in range(HEADS // 2):
            scores = dot(query_pair(p, hp), later_pair(1, p, hp), NT) + bias[hp][:, :ROWS]
            weights = jnp.exp(scores - jnp.max(scores, axis=-1, keepdims=True))
            att[4 * p + hp] = weights / jnp.sum(weights, axis=-1, keepdims=True)

    def backprop(p, cotangent, accumulate):
        d_attended = dot(cotangent, wproj_ref[...]).astype(BF)
        own = slice(ROWS * p, ROWS * (p + 1))
        parts = [[], [], []]
        for hp in range(HEADS // 2):
            d_pair = both(d_attended[:, 128 * hp:128 * (hp + 1)])
            attention = att[4 * p + hp]
            d_probs = dot(d_pair, later_pair(2, p, hp), NT)
            d_value = dot(attention.astype(BF), d_pair, TN)
            inner = jnp.sum(attention * d_probs, axis=-1, keepdims=True)
            d_scores = (attention * (d_probs - inner)).astype(BF)
            d_both = dot(d_scores, later_pair(1, p, hp))
            d_query = jnp.where(first_half, d_both[:ROWS], d_both[ROWS:]) * 0.125
            d_key = dot(d_scores, query_pair(p, hp), TN)
            for which, value in enumerate((d_query, d_key, d_value)):
                start = features * which + 128 * hp
                parts[which].append(value.astype(BF))
                at = (own, slice(start, start + 128))
                dqkv[at] = dqkv[at] + value if accumulate else value
        d_low = jnp.concatenate(parts[0] + parts[1] + parts[2], axis=1)
        d_normed = dot(d_low, wqkv_ref[...]) * gain
        return inv_std[own] * (
            d_normed
            - jnp.mean(d_normed, axis=-1, keepdims=True)
            - normed[own] * jnp.mean(d_normed * normed[own], axis=-1, keepdims=True))

    totals, skips = [], []
    for p in range(LEV):
        og_p = og[ROWS * p:ROWS * (p + 1)]
        totals.append(og_p + backprop(p, og_p.astype(BF), False))
        cot[p] = totals[p].astype(BF)
        skips.append(pltpu.make_async_remote_copy(
            cot.at[p], skip.at[p], skip_s.at[p], skip_r.at[p],
            device_id=(1 - ph, la, lo), device_id_type=MESH))
        pl.when(ph == 1)(skips[p].start)

    @pl.when(ph == 0)
    def _():
        for p in range(LEV):
            skips[p].wait_recv()
            received = skip[p]
            second = backprop(p, received, True)
            cot[p] = (totals[p] + (received.astype(F32) + second)).astype(BF)

    for l in range(n_lat):
        low[l] = dqkv[:, cols * l:cols * (l + 1)].astype(BF)
    low_copies = []
    for d in range(1, n_lat):
        to = device(d, 0)
        low_copies.append(pltpu.make_async_remote_copy(
            low.at[to[1]], low_in.at[d - 1], low_s.at[d - 1], low_r.at[d - 1],
            device_id=to, device_id_type=MESH))
        low_copies[-1].start()

    whole = cot[...].reshape(WROWS, features)
    back_src[...] = dot(to_win, whole, TN).astype(BF).reshape(LAT, LON, LEV, features)
    back = []
    for ih, jh in ((0, 0), (0, 1), (1, 0)):
        k = len(back)
        back.append(pltpu.make_async_remote_copy(
            quadrant(back_src, 1 - ih, 1 - jh), quadrant(gin_ref, ih, jh), back_s.at[k], back_r.at[k],
            device_id=device(1 - ih, 1 - jh), device_id_type=MESH))
    gin_ref[LAT // 2:, LON // 2:] = back_src[:LAT // 2, :LON // 2]

    for copy in sc_copies + low_copies:
        copy.wait()
    pair_to = (ph, la, lo + 1 - 2 * par)
    pairs = []
    for c in range(chunks):
        at = slice(chunk * c, chunk * (c + 1))
        value = dot(scaled[...], low[la][:, at], TN)
        for d in range(1, n_lat):
            value = value + dot(scaled_in[d - 1], low_in[d - 1][:, at], TN)
        value = value.astype(BF)
        for j in range(n_lon):
            part[c, j % 2, j // 2] = value[rows * j:rows * (j + 1)]
        pairs.append(pltpu.make_async_remote_copy(
            part.at[c, 1 - par], part_in.at[c], pair_s.at[c], pair_r.at[c],
            device_id=pair_to, device_id_type=MESH))
        pairs[-1].start()
    for copy in back:
        copy.start()
    groups = []
    for c in range(chunks):
        pairs[c].wait_recv()
        summed[c] = (part[c, par].astype(F32) + part_in[c].astype(F32)).astype(BF)
        for d in range(1, half):
            to = lax.rem(grp + d, half)
            groups.append(pltpu.make_async_remote_copy(
                summed.at[c, to], summed_in.at[c, d - 1],
                grp_s.at[c, d - 1], grp_r.at[c, d - 1],
                device_id=(ph, la, 2 * to + par), device_id_type=MESH))
            groups[-1].start()

    for copy in groups:
        copy.wait()
    for c in range(chunks):
        value = summed[c, grp].astype(F32)
        for d in range(1, half):
            value = value + summed_in[c, d - 1].astype(F32)
        gq_ref[:, chunk * c:chunk * (c + 1)] = value
    for copy in pairs:
        copy.wait_send()
    for copy in back:
        copy.wait()

    @pl.when(ph == 1)
    def _():
        for copy in skips:
            copy.wait_send()


def cells_first(field):
    return field[0].transpose(1, 2, 0, 3)


def per_device(n_lat, n_lon, x_in, out_grad, w_qkv, w_proj, norm_gain, bias_table, lat_labels):
    features = x_in.shape[-1]
    outs = w_qkv.shape[1]
    cols, rows = outs // n_lat, features // n_lon
    chunk = 256 if cols % 256 == 0 else cols
    chunks, half = cols // chunk, n_lon // 2
    vmem = pl.BlockSpec(memory_space=pltpu.VMEM)
    dma = lambda *shape: pltpu.SemaphoreType.DMA(shape)
    peers = max(n_lat - 1, 1)
    grid = (LAT, LON, LEV, features)
    grad_input, grad_qkv = pl.pallas_call(
        functools.partial(kernel, n_lat, n_lon, chunk),
        out_shape=(
            jax.ShapeDtypeStruct(grid, BF),
            jax.ShapeDtypeStruct((rows, cols), F32),
        ),
        in_specs=[pl.BlockSpec(memory_space=pl.ANY)] * 8,
        out_specs=(vmem, vmem),
        scratch_shapes=[
            pltpu.VMEM(grid, BF),
            pltpu.VMEM(grid, BF),
            pltpu.VMEM((outs, features), BF),
            pltpu.VMEM((features, features), BF),
            pltpu.VMEM((1, features), F32),
            pltpu.VMEM(bias_table.shape[1:], F32),
            pltpu.SMEM((LAT,), jnp.int32),
            pltpu.VMEM((WROWS + 256, 256), F32),
            pltpu.VMEM((8, 128), F32),
            pltpu.VMEM((8, 128), F32),
            pltpu.VMEM((8 * CELLS, 128), F32),
            pltpu.VMEM((8 * CELLS, 128), F32),
            pltpu.VMEM((HEADS // 2, 2 * ROWS, 128), F32),
            pltpu.VMEM((WROWS, outs), BF),
            pltpu.VMEM((HEADS, 2 * ROWS, ROWS), F32),
            pltpu.VMEM((WROWS, outs), F32),
            pltpu.VMEM((LEV, ROWS, features), BF),
            pltpu.VMEM((LEV, ROWS, features), BF),
            pltpu.VMEM(grid, BF),
            pltpu.VMEM((WROWS, features), BF),
            pltpu.VMEM((peers, WROWS, features), BF),
            pltpu.VMEM((n_lat, WROWS, cols), BF),
            pltpu.VMEM((peers, WROWS, cols), BF),
            pltpu.VMEM((chunks, 2, half, rows, chunk), BF),
            pltpu.VMEM((chunks, half, rows, chunk), BF),
            pltpu.VMEM((chunks, half, rows, chunk), BF),
            pltpu.VMEM((chunks, half - 1, rows, chunk), BF),
            dma(8), dma(6), dma(6), dma(1), dma(1), dma(LEV), dma(LEV), dma(3), dma(3),
            dma(peers), dma(peers), dma(peers), dma(peers),
            dma(chunks), dma(chunks), dma(chunks, half - 1), dma(chunks, half - 1),
        ],
        compiler_params=pltpu.CompilerParams(
            collective_id=0, has_side_effects=True, vmem_limit_bytes=60 * 1024 * 1024),
    )(
        cells_first(x_in), cells_first(out_grad), w_qkv[0], w_proj[0], norm_gain,
        bias_table[0], lat_labels, jnp.asarray(selections()))
    return grad_input.transpose(2, 0, 1, 3)[None], grad_qkv.T[None]


def solution(mesh):
    in_specs = (
        P("phase", None, "lat", "lon", None),
        P("phase", None, "lat", "lon", None),
        P("phase", None, None),
        P("phase", None, None),
        P("phase", None),
        P("phase", None, None),
        P("lat"),
    )
    out_specs = (P("phase", None, "lat", "lon", None), P("phase", "lat", "lon"))
    return jax.shard_map(
        functools.partial(per_device, mesh.shape["lat"], mesh.shape["lon"]),
        mesh=mesh, in_specs=in_specs, out_specs=out_specs, check_vma=False)
```

```python
import functools

import jax
import jax.numpy as jnp
import numpy as np
from jax import lax
from jax.experimental import pallas as pl
from jax.experimental.pallas import tpu as pltpu
from jax.sharding import PartitionSpec as P

HEADS = 8
EPSILON = 1e-05
MASKED = -1e30
MESH = pl.DeviceIdType.MESH
BF = jnp.bfloat16
F32 = jnp.float32

LEV, LAT, LON = 2, 6, 12
CELLS = LAT * LON
ROWS = 80
WROWS = LEV * ROWS


def selections():
    packed = np.zeros((WROWS + 256, 256), np.float32)
    for n in range(CELLS):
        i, j = divmod(n, LON)
        for p in range(LEV):
            packed[ROWS * (1 - p) + n, LEV * n + p] = 1
        packed[WROWS + 126 - (23 * i + j), n] = 1
        packed[WROWS + 128 + (i + 3) % 6, n] = 1
    return packed


def steps(features, cols, chunk, n_lat):
    order, last = [], []
    for l in range(n_lat):
        starts = range(cols * l, cols * (l + 1), chunk)
        pair = {
            start: max(c % features for c in range(start, start + chunk, 64)) // 128
            for start in starts
        }
        order.append(sorted(starts, key=lambda start: pair[start]))
        last.append([pair[start] for start in order[-1]])
    if chunk != 128:
        return order, [HEADS // 2 - 1] * (cols // chunk)
    return order, [max(step) for step in zip(*last)]


def dot(a, b, dims=((1,), (0,))):
    return lax.dot_general(a, b, (dims, ((), ())), preferred_element_type=F32)


NT = ((1,), (1,))
TN = ((0,), (0,))


def kernel(
    n_lat, n_lon, chunk, order, ready,
    x_hbm, og_hbm, wqkv_hbm, wproj_hbm, gain_hbm, table_hbm, labels_hbm, select_hbm,
    gin_ref, gq_ref,
    win_x, win_og, wqkv_ref, wproj_ref, gain_ref, table_ref, labels_ref, select_ref,
    send_lab, recv_lab, rolled, expanded, bias, proj, att, dqkv, cot, skip, back_src,
    scaled, scaled_in, turned, low, low_in, part, part_in, summed, summed_in,
    local_s, halo_s, halo_r, lab_s, lab_r, skip_s, skip_r, back_s, back_r,
    sc_s, sc_r, low_s, low_r, pair_s, pair_r, grp_s, grp_r,
):
    ph, la, lo = lax.axis_index("phase"), lax.axis_index("lat"), lax.axis_index("lon")
    features = gain_ref.shape[-1]
    rows, cols = gq_ref.shape
    half = n_lon // 2
    chunks = cols // chunk
    par = lax.rem(lo, 2)
    grp = lo // 2

    def device(dlat, dlon):
        return (ph, lax.rem(la + dlat + n_lat, n_lat), lax.rem(lo + dlon + n_lon, n_lon))

    offsets = set()
    for dlat, dlon in ((0, 1), (1, 0), (1, 1)):
        offsets |= {(dlat % n_lat, dlon % n_lon), (-dlat % n_lat, -dlon % n_lon)}
    offsets |= {(d, 0) for d in range(1, n_lat)}
    offsets |= {(0, 2 * d) for d in range(1, half)}
    offsets = sorted(offsets)
    barrier = pltpu.get_barrier_semaphore()
    for dlat, dlon in offsets:
        pl.semaphore_signal(barrier, inc=1, device_id=device(dlat, dlon), device_id_type=MESH)
    pl.semaphore_signal(barrier, inc=1, device_id=(1 - ph, la, lo), device_id_type=MESH)

    def quadrant(ref, ih, jh):
        return ref.at[pl.ds(ih * LAT // 2, LAT // 2), pl.ds(jh * LON // 2, LON // 2)]

    loads = []
    for k, (src, dst) in enumerate((
        (labels_hbm, labels_ref),
        (table_hbm, table_ref),
        (select_hbm, select_ref),
        (quadrant(x_hbm, 1, 1), quadrant(win_x, 0, 0)),
        (quadrant(og_hbm, 1, 1), quadrant(win_og, 0, 0)),
        (gain_hbm, gain_ref),
        (wqkv_hbm, wqkv_ref),
        (wproj_hbm, wproj_ref),
    )):
        loads.append(pltpu.make_async_copy(src, dst, local_s.at[k]))
        loads[-1].start()
    loads[0].wait()
    lane = lax.broadcasted_iota(jnp.int32, (8, 128), 1)
    own_lab = jnp.zeros((8, 128), F32)
    for i in range(LAT):
        own_lab = jnp.where(lane == i, labels_ref[i].astype(F32), own_lab)
    send_lab[...] = own_lab

    pl.semaphore_wait(barrier, len(offsets) + 1)

    halo = []
    for ih, jh in ((0, 0), (0, 1), (1, 0)):
        for src, dst in ((x_hbm, win_x), (og_hbm, win_og)):
            k = len(halo)
            halo.append(pltpu.make_async_remote_copy(
                quadrant(src, ih, jh), quadrant(dst, 1 - ih, 1 - jh), halo_s.at[k], halo_r.at[k],
                device_id=device(ih - 1, jh - 1), device_id_type=MESH))
            halo[-1].start()
    lab_copy = pltpu.make_async_remote_copy(
        send_lab, recv_lab, lab_s.at[0], lab_r.at[0],
        device_id=device(-1, 0), device_id_type=MESH)
    lab_copy.start()
    for copy in loads[1:3]:
        copy.wait()

    table = table_ref[:, 128:512]
    for m in range(CELLS):
        i, j = divmod(m, LON)
        shift = (384 - (125 + 23 * i + j)) % 384
        rolled[8 * m:8 * m + 8, :] = pltpu.roll(table, shift, 1)[:, :128]
    wide = rolled[...]
    high = wide.astype(BF)
    rest = wide - high.astype(F32)
    mid = rest.astype(BF)
    least = (rest - mid.astype(F32)).astype(BF)
    column = select_ref[WROWS:WROWS + 128, :128].astype(BF)
    expanded[...] = (dot(high, column) + dot(mid, column)) + dot(least, column)

    lab_copy.wait()
    lab = jnp.where(lane < 3, recv_lab[...], own_lab)
    lab_row = dot(jnp.concatenate([lab, lab], axis=0).astype(BF), select_ref[WROWS + 128:WROWS + 256, :128].astype(BF))[0:1]
    lane1 = lax.broadcasted_iota(jnp.int32, (1, 128), 1)
    lab_row = jnp.where(lane1 < CELLS, lab_row, -1.0)
    row_id = lax.broadcasted_iota(jnp.int32, (ROWS, 128), 0)
    lane_id = lax.broadcasted_iota(jnp.int32, (ROWS, 128), 1)
    want = jnp.zeros((ROWS, 128), jnp.int32)
    for i in range(LAT):
        want = jnp.where(row_id >= LON * i, (i + 3) % 6, want)
    lab_col = jnp.sum(jnp.where(lane_id == want, lab[0:1], 0.0), axis=1, keepdims=True)
    row1 = lax.broadcasted_iota(jnp.int32, (ROWS, 1), 0)
    lab_col = jnp.where(row1 < CELLS, lab_col, -1.0)
    allowed = lab_col == lab_row
    for h in range(HEADS):
        one = expanded[pl.ds(h, CELLS, stride=8), :]
        one = jnp.concatenate([one, jnp.zeros((ROWS - CELLS, 128), F32)], axis=0)
        bias[h // 2, ROWS * (h % 2):ROWS * (h % 2 + 1), :] = jnp.where(allowed, one, MASKED)

    for copy in loads[3:] + halo:
        copy.wait()
    to_win = select_ref[:WROWS, :LEV * CELLS].astype(BF)
    x = dot(to_win, win_x[...].reshape(LEV * CELLS, features))
    og = dot(to_win, win_og[...].reshape(LEV * CELLS, features))
    gain = gain_ref[...]
    center = jnp.mean(x, axis=-1, keepdims=True)
    spread = jnp.mean(jnp.square(x - center), axis=-1, keepdims=True)
    inv_std = lax.rsqrt(spread + EPSILON)
    normed = (x - center) * inv_std
    scaled[...] = (normed * gain).astype(BF)
    sc_copies = []
    for d in range(1, n_lat):
        sc_copies.append(pltpu.make_async_remote_copy(
            scaled, scaled_in.at[d - 1], sc_s.at[d - 1], sc_r.at[d - 1],
            device_id=device(d, 0), device_id_type=MESH))
        sc_copies[-1].start()
    proj[...] = dot(scaled[...], wqkv_ref[...], NT).astype(BF)
    first_half = lax.broadcasted_iota(jnp.int32, (ROWS, 128), 1) < 64
    zero = jnp.zeros((ROWS, 128), BF)

    def both(pair):
        return jnp.concatenate(
            [jnp.where(first_half, pair, zero), jnp.where(first_half, zero, pair)], axis=0)

    def query_pair(p, hp):
        pair = proj[ROWS * p:ROWS * (p + 1), 128 * hp:128 * (hp + 1)]
        return both(pair * jnp.asarray(0.125, BF))

    def later_pair(which, p, hp):
        start = features * which + 128 * hp
        return proj[ROWS * p:ROWS * (p + 1), start:start + 128]

    for p in range(LEV):
        for hp in range(HEADS // 2):
            scores = dot(query_pair(p, hp), later_pair(1, p, hp), NT) + bias[hp][:, :ROWS]
            weights = jnp.exp(scores - jnp.max(scores, axis=-1, keepdims=True))
            att[4 * p + hp] = weights / jnp.sum(weights, axis=-1, keepdims=True)

    def attended_grad(p, cotangent):
        return dot(cotangent, wproj_ref[...]).astype(BF)

    def attention_grad(p, hp, d_attended, accumulate):
        d_pair = both(d_attended[:, 128 * hp:128 * (hp + 1)])
        attention = att[4 * p + hp]
        d_probs = dot(d_pair, later_pair(2, p, hp), NT)
        d_value = dot(attention.astype(BF), d_pair, TN)
        inner = jnp.sum(attention * d_probs, axis=-1, keepdims=True)
        d_scores = (attention * (d_probs - inner)).astype(BF)
        d_both = dot(d_scores, later_pair(1, p, hp))
        d_query = jnp.where(first_half, d_both[:ROWS], d_both[ROWS:]) * 0.125
        d_key = dot(d_scores, query_pair(p, hp), TN)
        for which, value in enumerate((d_query, d_key, d_value)):
            start = features * which + 128 * hp
            at = (slice(ROWS * p, ROWS * (p + 1)), slice(start, start + 128))
            dqkv[at] = dqkv[at] + value if accumulate else value
        return [value.astype(BF) for value in (d_query, d_key, d_value)]

    def input_grad(p, parts):
        own = slice(ROWS * p, ROWS * (p + 1))
        d_low = jnp.concatenate([pair[w] for w in range(3) for pair in parts], axis=1)
        d_normed = dot(d_low, wqkv_ref[...]) * gain
        return inv_std[own] * (
            d_normed
            - jnp.mean(d_normed, axis=-1, keepdims=True)
            - normed[own] * jnp.mean(d_normed * normed[own], axis=-1, keepdims=True))

    totals, skips = [], []
    for p in range(LEV):
        og_p = og[ROWS * p:ROWS * (p + 1)]
        d_attended = attended_grad(p, og_p.astype(BF))
        parts = [attention_grad(p, hp, d_attended, False) for hp in range(HEADS // 2)]
        totals.append(og_p + input_grad(p, parts))
        cot[p] = totals[p].astype(BF)
        skips.append(pltpu.make_async_remote_copy(
            cot.at[p], skip.at[p], skip_s.at[p], skip_r.at[p],
            device_id=(1 - ph, la, lo), device_id_type=MESH))
        pl.when(ph == 1)(skips[p].start)

    turned[0] = scaled[...].T
    for d in range(1, n_lat):
        sc_copies[d - 1].wait()
        turned[d] = scaled_in[d - 1].T
    low_copies, pairs = [], []
    for c in range(chunks):
        low_copies.append([])
        for d in range(1, n_lat):
            to = device(d, 0)
            low_copies[c].append(pltpu.make_async_remote_copy(
                low.at[to[1], c], low_in.at[d - 1, c], low_s.at[d - 1, c], low_r.at[d - 1, c],
                device_id=to, device_id_type=MESH))
        pairs.append(pltpu.make_async_remote_copy(
            part.at[c, 1 - par], part_in.at[c], pair_s.at[c], pair_r.at[c],
            device_id=(ph, la, lo + 1 - 2 * par), device_id_type=MESH))

    def send_factors(c):
        for l in range(n_lat):
            low[l, c] = dqkv[:, order[l][c]:order[l][c] + chunk].astype(BF)
        for copy in low_copies[c]:
            copy.start()

    def send_sums(c):
        for copy in low_copies[c]:
            copy.wait_recv()
        value = dot(turned[0], low[la, c])
        for d in range(1, n_lat):
            value = value + dot(turned[d], low_in[d - 1, c])
        value = value.astype(BF)
        for j in range(n_lon):
            part[c, j % 2, j // 2] = value[rows * j:rows * (j + 1)]
        pairs[c].start()

    @pl.when(ph == 1)
    def _():
        for c in range(chunks):
            send_factors(c)
        for c in range(chunks):
            send_sums(c)

    @pl.when(ph == 0)
    def _():
        skips[0].wait_recv()
        d_attended = attended_grad(0, skip[0])
        all_parts = [[attention_grad(0, hp, d_attended, True) for hp in range(HEADS // 2)], []]
        skips[1].wait_recv()
        d_attended = attended_grad(1, skip[1])
        sent = 0
        for hp in range(HEADS // 2):
            all_parts[1].append(attention_grad(1, hp, d_attended, True))
            due = [c for c in range(chunks) if ready[c] == hp]
            for c in due:
                send_factors(c)
            while due and sent < due[0]:
                send_sums(sent)
                sent += 1
        while sent < chunks:
            send_sums(sent)
            sent += 1
        for p in range(LEV):
            second = input_grad(p, all_parts[p])
            cot[p] = (totals[p] + (skip[p].astype(F32) + second)).astype(BF)

    whole = cot[...].reshape(WROWS, features)
    back_src[...] = dot(to_win, whole, TN).astype(BF).reshape(LAT, LON, LEV, features)
    back = []
    for ih, jh in ((0, 0), (0, 1), (1, 0)):
        k = len(back)
        back.append(pltpu.make_async_remote_copy(
            quadrant(back_src, 1 - ih, 1 - jh), quadrant(gin_ref, ih, jh), back_s.at[k], back_r.at[k],
            device_id=device(1 - ih, 1 - jh), device_id_type=MESH))
    gin_ref[LAT // 2:, LON // 2:] = back_src[:LAT // 2, :LON // 2]

    for copy in back:
        copy.start()
    groups = []
    for c in range(chunks):
        pairs[c].wait_recv()
        summed[c] = (part[c, par].astype(F32) + part_in[c].astype(F32)).astype(BF)
        for d in range(1, half):
            to = lax.rem(grp + d, half)
            groups.append(pltpu.make_async_remote_copy(
                summed.at[c, to], summed_in.at[c, d - 1],
                grp_s.at[c, d - 1], grp_r.at[c, d - 1],
                device_id=(ph, la, 2 * to + par), device_id_type=MESH))
            groups[-1].start()

    for c in range(chunks):
        value = summed[c, grp].astype(F32)
        for d in range(1, half):
            groups[c * (half - 1) + d - 1].wait_recv()
            value = value + summed_in[c, d - 1].astype(F32)
        for l in range(n_lat):
            at = slice(order[l][c] - cols * l, order[l][c] - cols * l + chunk)

            @pl.when(la == l)
            def _(value=value, at=at):
                gq_ref[:, at] = value

    for copy in groups:
        copy.wait_send()
    for copy in pairs + [copy for step in low_copies for copy in step]:
        copy.wait_send()
    for copy in back:
        copy.wait()

    @pl.when(ph == 1)
    def _():
        for copy in skips:
            copy.wait_send()


def cells_first(field):
    return field[0].transpose(1, 2, 0, 3)


def finish(gin_hbm, gq_hbm, gin_out, gq_out, sems):
    copies = [
        pltpu.make_async_copy(gin_hbm, gin_out, sems.at[0]),
        pltpu.make_async_copy(gq_hbm, gq_out, sems.at[1]),
    ]
    for copy in copies:
        copy.start()
    for copy in copies:
        copy.wait()


def per_device(n_lat, n_lon, x_in, out_grad, w_qkv, w_proj, norm_gain, bias_table, lat_labels):
    features = x_in.shape[-1]
    outs = w_qkv.shape[1]
    cols, rows = outs // n_lat, features // n_lon
    chunk = 128 if cols % 128 == 0 else cols
    chunks, half = cols // chunk, n_lon // 2
    order, ready = steps(features, cols, chunk, n_lat)
    vmem = pl.BlockSpec(memory_space=pltpu.VMEM)
    dma = lambda *shape: pltpu.SemaphoreType.DMA(shape)
    peers = max(n_lat - 1, 1)
    grid = (LAT, LON, LEV, features)
    grad_input, grad_qkv = pl.pallas_call(
        functools.partial(kernel, n_lat, n_lon, chunk, order, ready),
        out_shape=(
            jax.ShapeDtypeStruct(grid, BF),
            jax.ShapeDtypeStruct((rows, cols), F32),
        ),
        in_specs=[pl.BlockSpec(memory_space=pl.ANY)] * 8,
        out_specs=(vmem, vmem),
        scratch_shapes=[
            pltpu.VMEM(grid, BF),
            pltpu.VMEM(grid, BF),
            pltpu.VMEM((outs, features), BF),
            pltpu.VMEM((features, features), BF),
            pltpu.VMEM((1, features), F32),
            pltpu.VMEM(bias_table.shape[1:], F32),
            pltpu.SMEM((LAT,), jnp.int32),
            pltpu.VMEM((WROWS + 256, 256), F32),
            pltpu.VMEM((8, 128), F32),
            pltpu.VMEM((8, 128), F32),
            pltpu.VMEM((8 * CELLS, 128), F32),
            pltpu.VMEM((8 * CELLS, 128), F32),
            pltpu.VMEM((HEADS // 2, 2 * ROWS, 128), F32),
            pltpu.VMEM((WROWS, outs), BF),
            pltpu.VMEM((HEADS, 2 * ROWS, ROWS), F32),
            pltpu.VMEM((WROWS, outs), F32),
            pltpu.VMEM((LEV, ROWS, features), BF),
            pltpu.VMEM((LEV, ROWS, features), BF),
            pltpu.VMEM(grid, BF),
            pltpu.VMEM((WROWS, features), BF),
            pltpu.VMEM((peers, WROWS, features), BF),
            pltpu.VMEM((n_lat, features, WROWS), BF),
            pltpu.VMEM((n_lat, chunks, WROWS, chunk), BF),
            pltpu.VMEM((peers, chunks, WROWS, chunk), BF),
            pltpu.VMEM((chunks, 2, half, rows, chunk), BF),
            pltpu.VMEM((chunks, half, rows, chunk), BF),
            pltpu.VMEM((chunks, half, rows, chunk), BF),
            pltpu.VMEM((chunks, half - 1, rows, chunk), BF),
            dma(8), dma(6), dma(6), dma(1), dma(1), dma(LEV), dma(LEV), dma(3), dma(3),
            dma(peers), dma(peers), dma(peers, chunks), dma(peers, chunks),
            dma(chunks), dma(chunks), dma(chunks, half - 1), dma(chunks, half - 1),
        ],
        compiler_params=pltpu.CompilerParams(
            collective_id=0, has_side_effects=True, vmem_limit_bytes=60 * 1024 * 1024),
    )(
        cells_first(x_in), cells_first(out_grad), w_qkv[0], w_proj[0], norm_gain,
        bias_table[0], lat_labels, jnp.asarray(selections()))
    grad_input, grad_qkv = pl.pallas_call(
        finish,
        out_shape=(
            jax.ShapeDtypeStruct(grid, BF),
            jax.ShapeDtypeStruct((rows, cols), F32),
        ),
        in_specs=[pl.BlockSpec(memory_space=pl.ANY)] * 2,
        out_specs=[pl.BlockSpec(memory_space=pl.ANY)] * 2,
        scratch_shapes=[pltpu.SemaphoreType.DMA((2,))],
    )(grad_input, grad_qkv)
    return grad_input.transpose(2, 0, 1, 3)[None], grad_qkv.T[None]


def solution(mesh):
    in_specs = (
        P("phase", None, "lat", "lon", None),
        P("phase", None, "lat", "lon", None),
        P("phase", None, None),
        P("phase", None, None),
        P("phase", None),
        P("phase", None, None),
        P("lat"),
    )
    out_specs = (P("phase", None, "lat", "lon", None), P("phase", "lat", "lon"))
    return jax.shard_map(
        functools.partial(per_device, mesh.shape["lat"], mesh.shape["lon"]),
        mesh=mesh, in_specs=in_specs, out_specs=out_specs, check_vma=False)
```

```python
import functools

import jax
import jax.numpy as jnp
import numpy as np
from jax import lax
from jax.experimental import pallas as pl
from jax.experimental.pallas import tpu as pltpu
from jax.sharding import PartitionSpec as P

HEADS = 8
EPSILON = 1e-05
MASKED = -1e30
MESH = pl.DeviceIdType.MESH
BF = jnp.bfloat16
F32 = jnp.float32

LEV, LAT, LON = 2, 6, 12
CELLS = LAT * LON
ROWS = 80
WROWS = LEV * ROWS


def selections():
    packed = np.zeros((WROWS + 256, 256), np.float32)
    for n in range(CELLS):
        i, j = divmod(n, LON)
        for p in range(LEV):
            packed[ROWS * (1 - p) + n, LEV * n + p] = 1
        packed[WROWS + 126 - (23 * i + j), n] = 1
        packed[WROWS + 128 + (i + 3) % 6, n] = 1
    return packed


def dot(a, b, dims=((1,), (0,))):
    return lax.dot_general(a, b, (dims, ((), ())), preferred_element_type=F32)


NT = ((1,), (1,))
TN = ((0,), (0,))


def kernel(
    n_lat, n_lon, chunk,
    x_hbm, og_hbm, wqkv_hbm, wproj_hbm, gain_hbm, table_hbm, labels_hbm, select_hbm,
    gin_ref, gq_ref,
    win_x, win_og, wqkv_ref, wproj_ref, gain_ref, table_ref, labels_ref, select_ref,
    send_lab, recv_lab, rolled, expanded, bias, proj, att, dqkv, cot, skip, back_src,
    scaled, scaled_in, turned, low, low_in, part, part_in, summed, summed_in,
    local_s, halo_s, halo_r, lab_s, lab_r, skip_s, skip_r, back_s, back_r,
    sc_s, sc_r, low_s, low_r, pair_s, pair_r, grp_s, grp_r,
):
    ph, la, lo = lax.axis_index("phase"), lax.axis_index("lat"), lax.axis_index("lon")
    features = gain_ref.shape[-1]
    rows, cols = gq_ref.shape
    half = n_lon // 2
    chunks = cols // chunk
    par = lax.rem(lo, 2)
    grp = lo // 2

    def device(dlat, dlon):
        return (ph, lax.rem(la + dlat + n_lat, n_lat), lax.rem(lo + dlon + n_lon, n_lon))

    offsets = set()
    for dlat, dlon in ((0, 1), (1, 0), (1, 1)):
        offsets |= {(dlat % n_lat, dlon % n_lon), (-dlat % n_lat, -dlon % n_lon)}
    offsets |= {(d, 0) for d in range(1, n_lat)}
    offsets |= {(0, 2 * d) for d in range(1, half)}
    offsets = sorted(offsets)
    barrier = pltpu.get_barrier_semaphore()
    for dlat, dlon in offsets:
        pl.semaphore_signal(barrier, inc=1, device_id=device(dlat, dlon), device_id_type=MESH)
    pl.semaphore_signal(barrier, inc=1, device_id=(1 - ph, la, lo), device_id_type=MESH)

    def quadrant(ref, ih, jh):
        return ref.at[pl.ds(ih * LAT // 2, LAT // 2), pl.ds(jh * LON // 2, LON // 2)]

    loads = []
    for k, (src, dst) in enumerate((
        (labels_hbm, labels_ref),
        (table_hbm, table_ref),
        (select_hbm, select_ref),
        (quadrant(x_hbm, 1, 1), quadrant(win_x, 0, 0)),
        (quadrant(og_hbm, 1, 1), quadrant(win_og, 0, 0)),
        (gain_hbm, gain_ref),
        (wqkv_hbm, wqkv_ref),
        (wproj_hbm, wproj_ref),
    )):
        loads.append(pltpu.make_async_copy(src, dst, local_s.at[k]))
        loads[-1].start()
    loads[0].wait()
    lane = lax.broadcasted_iota(jnp.int32, (8, 128), 1)
    own_lab = jnp.zeros((8, 128), F32)
    for i in range(LAT):
        own_lab = jnp.where(lane == i, labels_ref[i].astype(F32), own_lab)
    send_lab[...] = own_lab

    pl.semaphore_wait(barrier, len(offsets) + 1)

    halo = []
    for ih, jh in ((0, 0), (0, 1), (1, 0)):
        for src, dst in ((x_hbm, win_x), (og_hbm, win_og)):
            k = len(halo)
            halo.append(pltpu.make_async_remote_copy(
                quadrant(src, ih, jh), quadrant(dst, 1 - ih, 1 - jh), halo_s.at[k], halo_r.at[k],
                device_id=device(ih - 1, jh - 1), device_id_type=MESH))
            halo[-1].start()
    lab_copy = pltpu.make_async_remote_copy(
        send_lab, recv_lab, lab_s.at[0], lab_r.at[0],
        device_id=device(-1, 0), device_id_type=MESH)
    lab_copy.start()
    for copy in loads[1:3]:
        copy.wait()

    table = table_ref[:, 128:512]
    for m in range(CELLS):
        i, j = divmod(m, LON)
        shift = (384 - (125 + 23 * i + j)) % 384
        rolled[8 * m:8 * m + 8, :] = pltpu.roll(table, shift, 1)[:, :128]
    wide = rolled[...]
    high = wide.astype(BF)
    rest = wide - high.astype(F32)
    mid = rest.astype(BF)
    least = (rest - mid.astype(F32)).astype(BF)
    column = select_ref[WROWS:WROWS + 128, :128].astype(BF)
    expanded[...] = (dot(high, column) + dot(mid, column)) + dot(least, column)

    lab_copy.wait()
    lab = jnp.where(lane < 3, recv_lab[...], own_lab)
    lab_row = dot(jnp.concatenate([lab, lab], axis=0).astype(BF), select_ref[WROWS + 128:WROWS + 256, :128].astype(BF))[0:1]
    lane1 = lax.broadcasted_iota(jnp.int32, (1, 128), 1)
    lab_row = jnp.where(lane1 < CELLS, lab_row, -1.0)
    row_id = lax.broadcasted_iota(jnp.int32, (ROWS, 128), 0)
    lane_id = lax.broadcasted_iota(jnp.int32, (ROWS, 128), 1)
    want = jnp.zeros((ROWS, 128), jnp.int32)
    for i in range(LAT):
        want = jnp.where(row_id >= LON * i, (i + 3) % 6, want)
    lab_col = jnp.sum(jnp.where(lane_id == want, lab[0:1], 0.0), axis=1, keepdims=True)
    row1 = lax.broadcasted_iota(jnp.int32, (ROWS, 1), 0)
    lab_col = jnp.where(row1 < CELLS, lab_col, -1.0)
    allowed = lab_col == lab_row
    for h in range(HEADS):
        one = expanded[pl.ds(h, CELLS, stride=8), :]
        one = jnp.concatenate([one, jnp.zeros((ROWS - CELLS, 128), F32)], axis=0)
        bias[h // 2, ROWS * (h % 2):ROWS * (h % 2 + 1), :] = jnp.where(allowed, one, MASKED)

    for copy in loads[3:] + halo:
        copy.wait()
    to_win = select_ref[:WROWS, :LEV * CELLS].astype(BF)
    x = dot(to_win, win_x[...].reshape(LEV * CELLS, features))
    og = dot(to_win, win_og[...].reshape(LEV * CELLS, features))
    gain = gain_ref[...]
    center = jnp.mean(x, axis=-1, keepdims=True)
    spread = jnp.mean(jnp.square(x - center), axis=-1, keepdims=True)
    inv_std = lax.rsqrt(spread + EPSILON)
    normed = (x - center) * inv_std
    scaled[...] = (normed * gain).astype(BF)
    sc_copies = []
    for d in range(1, n_lat):
        sc_copies.append(pltpu.make_async_remote_copy(
            scaled, scaled_in.at[d - 1], sc_s.at[d - 1], sc_r.at[d - 1],
            device_id=device(d, 0), device_id_type=MESH))
        sc_copies[-1].start()
    proj[...] = dot(scaled[...], wqkv_ref[...], NT).astype(BF)
    first_half = lax.broadcasted_iota(jnp.int32, (ROWS, 128), 1) < 64
    zero = jnp.zeros((ROWS, 128), BF)

    def both(pair):
        return jnp.concatenate(
            [jnp.where(first_half, pair, zero), jnp.where(first_half, zero, pair)], axis=0)

    def query_pair(p, hp):
        pair = proj[ROWS * p:ROWS * (p + 1), 128 * hp:128 * (hp + 1)]
        return both(pair * jnp.asarray(0.125, BF))

    def later_pair(which, p, hp):
        start = features * which + 128 * hp
        return proj[ROWS * p:ROWS * (p + 1), start:start + 128]

    pairs_of = range(HEADS // 2)
    units = [(p, hp) for p in range(LEV) for hp in pairs_of]
    scores = [
        dot(query_pair(p, hp), later_pair(1, p, hp), NT) + bias[hp][:, :ROWS] for p, hp in units]
    weights = [jnp.exp(s - jnp.max(s, axis=-1, keepdims=True)) for s in scores]
    scales = [1.0 / jnp.sum(w, axis=-1, keepdims=True) for w in weights]
    for k, (w, scale) in enumerate(zip(weights, scales)):
        att[k] = w * scale

    def attended_grad(p, cotangent):
        return dot(cotangent, wproj_ref[...]).astype(BF)

    def attention_grad(p, d_attended, accumulate):
        d_pairs = [both(d_attended[:, 128 * hp:128 * (hp + 1)]) for hp in pairs_of]
        d_probs = [dot(d_pairs[hp], later_pair(2, p, hp), NT) for hp in pairs_of]
        d_values = [dot(att[4 * p + hp].astype(BF), d_pairs[hp], TN) for hp in pairs_of]
        inner = [
            jnp.sum(att[4 * p + hp] * d_probs[hp], axis=-1, keepdims=True) for hp in pairs_of]
        d_scores = [
            (att[4 * p + hp] * (d_probs[hp] - inner[hp])).astype(BF) for hp in pairs_of]
        d_both = [dot(d_scores[hp], later_pair(1, p, hp)) for hp in pairs_of]
        d_keys = [dot(d_scores[hp], query_pair(p, hp), TN) for hp in pairs_of]
        d_queries = [jnp.where(first_half, d[:ROWS], d[ROWS:]) * 0.125 for d in d_both]
        values = d_queries + d_keys + d_values
        for k, value in enumerate(values):
            at = (slice(ROWS * p, ROWS * (p + 1)), slice(128 * k, 128 * (k + 1)))
            dqkv[at] = dqkv[at] + value if accumulate else value
        return [value.astype(BF) for value in values]

    def input_grad(p, lows):
        own = slice(ROWS * p, ROWS * (p + 1))
        d_normed = dot(jnp.concatenate(lows, axis=1), wqkv_ref[...]) * gain
        return inv_std[own] * (
            d_normed
            - jnp.mean(d_normed, axis=-1, keepdims=True)
            - normed[own] * jnp.mean(d_normed * normed[own], axis=-1, keepdims=True))

    totals, skips = [], []
    for p in range(LEV):
        og_p = og[ROWS * p:ROWS * (p + 1)]
        d_attended = attended_grad(p, og_p.astype(BF))
        totals.append(og_p + input_grad(p, attention_grad(p, d_attended, False)))
        cot[p] = totals[p].astype(BF)
        skips.append(pltpu.make_async_remote_copy(
            cot.at[p], skip.at[p], skip_s.at[p], skip_r.at[p],
            device_id=(1 - ph, la, lo), device_id_type=MESH))
        pl.when(ph == 1)(skips[p].start)

    turned[0] = scaled[...].T
    for d in range(1, n_lat):
        sc_copies[d - 1].wait()
        turned[d] = scaled_in[d - 1].T
    low_copies, pairs = [], []
    for c in range(chunks):
        low_copies.append([])
        for d in range(1, n_lat):
            to = device(d, 0)
            low_copies[c].append(pltpu.make_async_remote_copy(
                low.at[to[1], c], low_in.at[d - 1, c], low_s.at[d - 1, c], low_r.at[d - 1, c],
                device_id=to, device_id_type=MESH))
        pairs.append(pltpu.make_async_remote_copy(
            part.at[c, 1 - par], part_in.at[c], pair_s.at[c], pair_r.at[c],
            device_id=(ph, la, lo + 1 - 2 * par), device_id_type=MESH))

    def send_factors(c):
        for l in range(n_lat):
            start = cols * l + chunk * c
            low[l, c] = dqkv[:, start:start + chunk].astype(BF)
        for copy in low_copies[c]:
            copy.start()

    def send_sums(c):
        for copy in low_copies[c]:
            copy.wait_recv()
        value = dot(turned[0], low[la, c])
        for d in range(1, n_lat):
            value = value + dot(turned[d], low_in[d - 1, c])
        value = value.astype(BF)
        for j in range(n_lon):
            part[c, j % 2, j // 2] = value[rows * j:rows * (j + 1)]
        pairs[c].start()

    @pl.when(ph == 1)
    def _():
        for c in range(chunks):
            send_factors(c)
        for c in range(chunks):
            send_sums(c)

    @pl.when(ph == 0)
    def _():
        skips[0].wait_recv()
        d_attended = attended_grad(0, skip[0])
        all_lows = [attention_grad(0, d_attended, True)]
        skips[1].wait_recv()
        d_attended = attended_grad(1, skip[1])
        all_lows.append(attention_grad(1, d_attended, True))
        for c in range(chunks):
            send_factors(c)
        for c in range(chunks):
            send_sums(c)
        for p in range(LEV):
            second = input_grad(p, all_lows[p])
            cot[p] = (totals[p] + (skip[p].astype(F32) + second)).astype(BF)

    whole = cot[...].reshape(WROWS, features)
    back_src[...] = dot(to_win, whole, TN).astype(BF).reshape(LAT, LON, LEV, features)
    back = []
    for ih, jh in ((0, 0), (0, 1), (1, 0)):
        k = len(back)
        back.append(pltpu.make_async_remote_copy(
            quadrant(back_src, 1 - ih, 1 - jh), quadrant(gin_ref, ih, jh), back_s.at[k], back_r.at[k],
            device_id=device(1 - ih, 1 - jh), device_id_type=MESH))
    gin_ref[LAT // 2:, LON // 2:] = back_src[:LAT // 2, :LON // 2]

    for copy in back:
        copy.start()
    groups = []
    for c in range(chunks):
        pairs[c].wait_recv()
        summed[c] = (part[c, par].astype(F32) + part_in[c].astype(F32)).astype(BF)
        for d in range(1, half):
            to = lax.rem(grp + d, half)
            groups.append(pltpu.make_async_remote_copy(
                summed.at[c, to], summed_in.at[c, d - 1],
                grp_s.at[c, d - 1], grp_r.at[c, d - 1],
                device_id=(ph, la, 2 * to + par), device_id_type=MESH))
            groups[-1].start()

    for c in range(chunks):
        value = summed[c, grp].astype(F32)
        for d in range(1, half):
            groups[c * (half - 1) + d - 1].wait_recv()
            value = value + summed_in[c, d - 1].astype(F32)
        gq_ref[:, chunk * c:chunk * (c + 1)] = value

    for copy in groups:
        copy.wait_send()
    for copy in pairs + [copy for step in low_copies for copy in step]:
        copy.wait_send()
    for copy in back:
        copy.wait()

    @pl.when(ph == 1)
    def _():
        for copy in skips:
            copy.wait_send()


def cells_first(field):
    return field[0].transpose(1, 2, 0, 3)


def finish(gin_hbm, gq_hbm, gin_out, gq_out, gin_ref, gq_ref, in_sems, out_sems):
    halves = []
    for src, mid, dst in ((gin_hbm, gin_ref, gin_out), (gq_hbm, gq_ref, gq_out)):
        size = src.shape[0] // 2
        for k in range(2):
            at = pl.ds(size * k, size)
            n = len(halves)
            halves.append((
                pltpu.make_async_copy(src.at[at], mid.at[at], in_sems.at[n]),
                pltpu.make_async_copy(mid.at[at], dst.at[at], out_sems.at[n])))
    for load, _ in halves:
        load.start()
    for load, store in halves:
        load.wait()
        store.start()
    for _, store in halves:
        store.wait()


def per_device(n_lat, n_lon, x_in, out_grad, w_qkv, w_proj, norm_gain, bias_table, lat_labels):
    features = x_in.shape[-1]
    outs = w_qkv.shape[1]
    cols, rows = outs // n_lat, features // n_lon
    chunk = 128 if cols % 128 == 0 else cols
    chunks, half = cols // chunk, n_lon // 2
    vmem = pl.BlockSpec(memory_space=pltpu.VMEM)
    dma = lambda *shape: pltpu.SemaphoreType.DMA(shape)
    peers = max(n_lat - 1, 1)
    grid = (LAT, LON, LEV, features)
    grad_input, grad_qkv = pl.pallas_call(
        functools.partial(kernel, n_lat, n_lon, chunk),
        out_shape=(
            jax.ShapeDtypeStruct(grid, BF),
            jax.ShapeDtypeStruct((rows, cols), F32),
        ),
        in_specs=[pl.BlockSpec(memory_space=pl.ANY)] * 8,
        out_specs=(vmem, vmem),
        scratch_shapes=[
            pltpu.VMEM(grid, BF),
            pltpu.VMEM(grid, BF),
            pltpu.VMEM((outs, features), BF),
            pltpu.VMEM((features, features), BF),
            pltpu.VMEM((1, features), F32),
            pltpu.VMEM(bias_table.shape[1:], F32),
            pltpu.SMEM((LAT,), jnp.int32),
            pltpu.VMEM((WROWS + 256, 256), F32),
            pltpu.VMEM((8, 128), F32),
            pltpu.VMEM((8, 128), F32),
            pltpu.VMEM((8 * CELLS, 128), F32),
            pltpu.VMEM((8 * CELLS, 128), F32),
            pltpu.VMEM((HEADS // 2, 2 * ROWS, 128), F32),
            pltpu.VMEM((WROWS, outs), BF),
            pltpu.VMEM((HEADS, 2 * ROWS, ROWS), F32),
            pltpu.VMEM((WROWS, outs), F32),
            pltpu.VMEM((LEV, ROWS, features), BF),
            pltpu.VMEM((LEV, ROWS, features), BF),
            pltpu.VMEM(grid, BF),
            pltpu.VMEM((WROWS, features), BF),
            pltpu.VMEM((peers, WROWS, features), BF),
            pltpu.VMEM((n_lat, features, WROWS), BF),
            pltpu.VMEM((n_lat, chunks, WROWS, chunk), BF),
            pltpu.VMEM((peers, chunks, WROWS, chunk), BF),
            pltpu.VMEM((chunks, 2, half, rows, chunk), BF),
            pltpu.VMEM((chunks, half, rows, chunk), BF),
            pltpu.VMEM((chunks, half, rows, chunk), BF),
            pltpu.VMEM((chunks, half - 1, rows, chunk), BF),
            dma(8), dma(6), dma(6), dma(1), dma(1), dma(LEV), dma(LEV), dma(3), dma(3),
            dma(peers), dma(peers), dma(peers, chunks), dma(peers, chunks),
            dma(chunks), dma(chunks), dma(chunks, half - 1), dma(chunks, half - 1),
        ],
        compiler_params=pltpu.CompilerParams(
            collective_id=0, has_side_effects=True, vmem_limit_bytes=60 * 1024 * 1024),
    )(
        cells_first(x_in), cells_first(out_grad), w_qkv[0], w_proj[0], norm_gain,
        bias_table[0], lat_labels, jnp.asarray(selections()))
    grad_input, grad_qkv = pl.pallas_call(
        finish,
        out_shape=(
            jax.ShapeDtypeStruct(grid, BF),
            jax.ShapeDtypeStruct((rows, cols), F32),
        ),
        in_specs=[pl.BlockSpec(memory_space=pl.ANY)] * 2,
        out_specs=[pl.BlockSpec(memory_space=pl.ANY)] * 2,
        scratch_shapes=[
            pltpu.VMEM(grid, BF), pltpu.VMEM((rows, cols), F32), dma(4), dma(4)],
    )(grad_input, grad_qkv)
    return grad_input.transpose(2, 0, 1, 3)[None], grad_qkv.T[None]


def solution(mesh):
    in_specs = (
        P("phase", None, "lat", "lon", None),
        P("phase", None, "lat", "lon", None),
        P("phase", None, None),
        P("phase", None, None),
        P("phase", None),
        P("phase", None, None),
        P("lat"),
    )
    out_specs = (P("phase", None, "lat", "lon", None), P("phase", "lat", "lon"))
    return jax.shard_map(
        functools.partial(per_device, mesh.shape["lat"], mesh.shape["lon"]),
        mesh=mesh, in_specs=in_specs, out_specs=out_specs, check_vma=False)
```

```python
import functools

import jax
import jax.numpy as jnp
import numpy as np
from jax import lax
from jax.experimental import pallas as pl
from jax.experimental.pallas import tpu as pltpu
from jax.sharding import PartitionSpec as P

HEADS = 8
EPSILON = 1e-05
MASKED = -1e30
MESH = pl.DeviceIdType.MESH
BF = jnp.bfloat16
F32 = jnp.float32

LEV, LAT, LON = 2, 6, 12
CELLS = LAT * LON
ROWS = 80
WROWS = LEV * ROWS


def selections():
    packed = np.zeros((WROWS + 256, 256), np.float32)
    for n in range(CELLS):
        i, j = divmod(n, LON)
        for p in range(LEV):
            packed[ROWS * (1 - p) + n, LEV * n + p] = 1
        packed[WROWS + 126 - (23 * i + j), n] = 1
        packed[WROWS + 128 + (i + 3) % 6, n] = 1
    return packed


def dot(a, b, dims=((1,), (0,))):
    return lax.dot_general(a, b, (dims, ((), ())), preferred_element_type=F32)


NT = ((1,), (1,))
TN = ((0,), (0,))


def kernel(
    n_lat, n_lon, chunk,
    x_hbm, og_hbm, wqkv_hbm, wproj_hbm, gain_hbm, table_hbm, labels_hbm, select_hbm,
    gin_ref, gq_ref,
    win_x, win_og, wqkv_ref, wproj_ref, gain_ref, table_ref, labels_ref, select_ref,
    send_lab, recv_lab, rolled, expanded, bias, proj, att, dqkv, cot, skip, back_src,
    scaled, scaled_in, turned, low, low_in, part, part_in, summed, summed_in,
    local_s, halo_s, halo_r, lab_s, lab_r, skip_s, skip_r, back_s, back_r,
    sc_s, sc_r, low_s, low_r, pair_s, pair_r, grp_s, grp_r,
):
    ph, la, lo = lax.axis_index("phase"), lax.axis_index("lat"), lax.axis_index("lon")
    features = gain_ref.shape[-1]
    rows, cols = gq_ref.shape
    half = n_lon // 2
    chunks = cols // chunk
    par = lax.rem(lo, 2)
    grp = lo // 2

    def device(dlat, dlon):
        return (ph, lax.rem(la + dlat + n_lat, n_lat), lax.rem(lo + dlon + n_lon, n_lon))

    offsets = set()
    for dlat, dlon in ((0, 1), (1, 0), (1, 1)):
        offsets |= {(dlat % n_lat, dlon % n_lon), (-dlat % n_lat, -dlon % n_lon)}
    offsets |= {(d, 0) for d in range(1, n_lat)}
    offsets |= {(0, 2 * d) for d in range(1, half)}
    offsets = sorted(offsets)
    barrier = pltpu.get_barrier_semaphore()
    for dlat, dlon in offsets:
        pl.semaphore_signal(barrier, inc=1, device_id=device(dlat, dlon), device_id_type=MESH)
    pl.semaphore_signal(barrier, inc=1, device_id=(1 - ph, la, lo), device_id_type=MESH)

    def quadrant(ref, ih, jh):
        return ref.at[pl.ds(ih * LAT // 2, LAT // 2), pl.ds(jh * LON // 2, LON // 2)]

    loads = []
    for k, (src, dst) in enumerate((
        (labels_hbm, labels_ref),
        (table_hbm, table_ref),
        (select_hbm, select_ref),
        (quadrant(x_hbm, 1, 1), quadrant(win_x, 0, 0)),
        (gain_hbm, gain_ref),
        (wqkv_hbm, wqkv_ref),
        (quadrant(og_hbm, 1, 1), quadrant(win_og, 0, 0)),
        (wproj_hbm, wproj_ref),
    )):
        loads.append(pltpu.make_async_copy(src, dst, local_s.at[k]))
        loads[-1].start()
    pl.semaphore_wait(barrier, len(offsets) + 1)

    halo = []
    for src, dst in ((x_hbm, win_x), (og_hbm, win_og)):
        for ih, jh in ((0, 0), (1, 0), (0, 1)):
            k = len(halo)
            halo.append(pltpu.make_async_remote_copy(
                quadrant(src, ih, jh), quadrant(dst, 1 - ih, 1 - jh), halo_s.at[k], halo_r.at[k],
                device_id=device(ih - 1, jh - 1), device_id_type=MESH))
            halo[-1].start()
    loads[0].wait()
    lane = lax.broadcasted_iota(jnp.int32, (8, 128), 1)
    own_lab = jnp.zeros((8, 128), F32)
    for i in range(LAT):
        own_lab = jnp.where(lane == i, labels_ref[i].astype(F32), own_lab)
    send_lab[...] = own_lab

    lab_copy = pltpu.make_async_remote_copy(
        send_lab, recv_lab, lab_s.at[0], lab_r.at[0],
        device_id=device(-1, 0), device_id_type=MESH)
    lab_copy.start()
    for copy in loads[1:3]:
        copy.wait()

    table = table_ref[:, 128:512]
    for m in range(CELLS):
        i, j = divmod(m, LON)
        shift = (384 - (125 + 23 * i + j)) % 384
        rolled[8 * m:8 * m + 8, :] = pltpu.roll(table, shift, 1)[:, :128]
    wide = rolled[...]
    high = wide.astype(BF)
    rest = wide - high.astype(F32)
    mid = rest.astype(BF)
    least = (rest - mid.astype(F32)).astype(BF)
    column = select_ref[WROWS:WROWS + 128, :128].astype(BF)
    expanded[...] = (dot(high, column) + dot(mid, column)) + dot(least, column)

    lab_copy.wait()
    lab = jnp.where(lane < 3, recv_lab[...], own_lab)
    lab_row = dot(jnp.concatenate([lab, lab], axis=0).astype(BF), select_ref[WROWS + 128:WROWS + 256, :128].astype(BF))[0:1]
    lane1 = lax.broadcasted_iota(jnp.int32, (1, 128), 1)
    lab_row = jnp.where(lane1 < CELLS, lab_row, -1.0)
    row_id = lax.broadcasted_iota(jnp.int32, (ROWS, 128), 0)
    lane_id = lax.broadcasted_iota(jnp.int32, (ROWS, 128), 1)
    want = jnp.zeros((ROWS, 128), jnp.int32)
    for i in range(LAT):
        want = jnp.where(row_id >= LON * i, (i + 3) % 6, want)
    lab_col = jnp.sum(jnp.where(lane_id == want, lab[0:1], 0.0), axis=1, keepdims=True)
    row1 = lax.broadcasted_iota(jnp.int32, (ROWS, 1), 0)
    lab_col = jnp.where(row1 < CELLS, lab_col, -1.0)
    allowed = lab_col == lab_row
    for h in range(HEADS):
        one = expanded[pl.ds(h, CELLS, stride=8), :]
        one = jnp.concatenate([one, jnp.zeros((ROWS - CELLS, 128), F32)], axis=0)
        bias[h // 2, ROWS * (h % 2):ROWS * (h % 2 + 1), :] = jnp.where(allowed, one, MASKED)

    for copy in loads[3:6] + halo[:3]:
        copy.wait()
    to_win = select_ref[:WROWS, :LEV * CELLS].astype(BF)
    x = dot(to_win, win_x[...].reshape(LEV * CELLS, features))
    gain = gain_ref[...]
    center = jnp.mean(x, axis=-1, keepdims=True)
    spread = jnp.mean(jnp.square(x - center), axis=-1, keepdims=True)
    inv_std = lax.rsqrt(spread + EPSILON)
    normed = (x - center) * inv_std
    scaled[...] = (normed * gain).astype(BF)
    sc_copies = []
    for d in range(1, n_lat):
        sc_copies.append(pltpu.make_async_remote_copy(
            scaled, scaled_in.at[d - 1], sc_s.at[d - 1], sc_r.at[d - 1],
            device_id=device(d, 0), device_id_type=MESH))
        sc_copies[-1].start()
    proj[...] = dot(scaled[...], wqkv_ref[...], NT).astype(BF)
    first_half = lax.broadcasted_iota(jnp.int32, (ROWS, 128), 1) < 64
    zero = jnp.zeros((ROWS, 128), BF)

    def both(pair):
        return jnp.concatenate(
            [jnp.where(first_half, pair, zero), jnp.where(first_half, zero, pair)], axis=0)

    def query_pair(p, hp):
        pair = proj[ROWS * p:ROWS * (p + 1), 128 * hp:128 * (hp + 1)]
        return both(pair * jnp.asarray(0.125, BF))

    def later_pair(which, p, hp):
        start = features * which + 128 * hp
        return proj[ROWS * p:ROWS * (p + 1), start:start + 128]

    pairs_of = range(HEADS // 2)
    units = [(p, hp) for p in range(LEV) for hp in pairs_of]
    scores = [
        dot(query_pair(p, hp), later_pair(1, p, hp), NT) + bias[hp][:, :ROWS] for p, hp in units]
    weights = [jnp.exp(s - jnp.max(s, axis=-1, keepdims=True)) for s in scores]
    scales = [1.0 / jnp.sum(w, axis=-1, keepdims=True) for w in weights]
    for k, (w, scale) in enumerate(zip(weights, scales)):
        att[k] = w * scale

    def attended_grad(p, cotangent):
        return dot(cotangent, wproj_ref[...]).astype(BF)

    def attention_grad(p, d_attended, accumulate):
        d_pairs = [both(d_attended[:, 128 * hp:128 * (hp + 1)]) for hp in pairs_of]
        d_probs = [dot(d_pairs[hp], later_pair(2, p, hp), NT) for hp in pairs_of]
        d_values = [dot(att[4 * p + hp].astype(BF), d_pairs[hp], TN) for hp in pairs_of]
        inner = [
            jnp.sum(att[4 * p + hp] * d_probs[hp], axis=-1, keepdims=True) for hp in pairs_of]
        d_scores = [
            (att[4 * p + hp] * (d_probs[hp] - inner[hp])).astype(BF) for hp in pairs_of]
        d_both = [dot(d_scores[hp], later_pair(1, p, hp)) for hp in pairs_of]
        d_keys = [dot(d_scores[hp], query_pair(p, hp), TN) for hp in pairs_of]
        d_queries = [jnp.where(first_half, d[:ROWS], d[ROWS:]) * 0.125 for d in d_both]
        values = d_queries + d_keys + d_values
        for k, value in enumerate(values):
            at = (slice(ROWS * p, ROWS * (p + 1)), slice(128 * k, 128 * (k + 1)))
            dqkv[at] = dqkv[at] + value if accumulate else value
        return [value.astype(BF) for value in values]

    def input_grad(p, lows):
        own = slice(ROWS * p, ROWS * (p + 1))
        d_normed = dot(jnp.concatenate(lows, axis=1), wqkv_ref[...]) * gain
        return inv_std[own] * (
            d_normed
            - jnp.mean(d_normed, axis=-1, keepdims=True)
            - normed[own] * jnp.mean(d_normed * normed[own], axis=-1, keepdims=True))

    for copy in loads[6:] + halo[3:]:
        copy.wait()
    og = dot(to_win, win_og[...].reshape(LEV * CELLS, features))
    totals, skips = [], []
    for p in range(LEV):
        og_p = og[ROWS * p:ROWS * (p + 1)]
        d_attended = attended_grad(p, og_p.astype(BF))
        totals.append(og_p + input_grad(p, attention_grad(p, d_attended, False)))
        cot[p] = totals[p].astype(BF)
        skips.append(pltpu.make_async_remote_copy(
            cot.at[p], skip.at[p], skip_s.at[p], skip_r.at[p],
            device_id=(1 - ph, la, lo), device_id_type=MESH))
        pl.when(ph == 1)(skips[p].start)

    turned[0] = scaled[...].T
    for d in range(1, n_lat):
        sc_copies[d - 1].wait()
        turned[d] = scaled_in[d - 1].T
    low_copies, pairs = [], []
    for c in range(chunks):
        low_copies.append([])
        for d in range(1, n_lat):
            to = device(d, 0)
            low_copies[c].append(pltpu.make_async_remote_copy(
                low.at[to[1], c], low_in.at[d - 1, c], low_s.at[d - 1, c], low_r.at[d - 1, c],
                device_id=to, device_id_type=MESH))
        pairs.append(pltpu.make_async_remote_copy(
            part.at[c, 1 - par], part_in.at[c], pair_s.at[c], pair_r.at[c],
            device_id=(ph, la, lo + 1 - 2 * par), device_id_type=MESH))

    def send_factors(c):
        for l in range(n_lat):
            start = cols * l + chunk * c
            low[l, c] = dqkv[:, start:start + chunk].astype(BF)
        for copy in low_copies[c]:
            copy.start()

    def send_sums(c):
        for copy in low_copies[c]:
            copy.wait_recv()
        value = dot(turned[0], low[la, c])
        for d in range(1, n_lat):
            value = value + dot(turned[d], low_in[d - 1, c])
        value = value.astype(BF)
        for j in range(n_lon):
            part[c, j % 2, j // 2] = value[rows * j:rows * (j + 1)]
        pairs[c].start()

    @pl.when(ph == 1)
    def _():
        for c in range(chunks):
            send_factors(c)
        for c in range(chunks):
            send_sums(c)

    @pl.when(ph == 0)
    def _():
        skips[0].wait_recv()
        d_attended = attended_grad(0, skip[0])
        lows = attention_grad(0, d_attended, True)
        cot[0] = (totals[0] + (skip[0].astype(F32) + input_grad(0, lows))).astype(BF)
        skips[1].wait_recv()
        d_attended = attended_grad(1, skip[1])
        lows = attention_grad(1, d_attended, True)
        for c in range(chunks):
            send_factors(c)
        cot[1] = (totals[1] + (skip[1].astype(F32) + input_grad(1, lows))).astype(BF)
        for c in range(chunks):
            send_sums(c)

    whole = cot[...].reshape(WROWS, features)
    back_src[...] = dot(to_win, whole, TN).astype(BF).reshape(LAT, LON, LEV, features)
    back = []
    for ih, jh in ((0, 0), (0, 1), (1, 0)):
        k = len(back)
        back.append(pltpu.make_async_remote_copy(
            quadrant(back_src, 1 - ih, 1 - jh), quadrant(gin_ref, ih, jh), back_s.at[k], back_r.at[k],
            device_id=device(1 - ih, 1 - jh), device_id_type=MESH))
    gin_ref[LAT // 2:, LON // 2:] = back_src[:LAT // 2, :LON // 2]

    for copy in back:
        copy.start()
    groups = []
    for c in range(chunks):
        pairs[c].wait_recv()
        summed[c] = (part[c, par].astype(F32) + part_in[c].astype(F32)).astype(BF)
        for d in range(1, half):
            to = lax.rem(grp + d, half)
            groups.append(pltpu.make_async_remote_copy(
                summed.at[c, to], summed_in.at[c, d - 1],
                grp_s.at[c, d - 1], grp_r.at[c, d - 1],
                device_id=(ph, la, 2 * to + par), device_id_type=MESH))
            groups[-1].start()

    for c in range(chunks):
        value = summed[c, grp].astype(F32)
        for d in range(1, half):
            groups[c * (half - 1) + d - 1].wait_recv()
            value = value + summed_in[c, d - 1].astype(F32)
        gq_ref[:, chunk * c:chunk * (c + 1)] = value

    for copy in groups:
        copy.wait_send()
    for copy in pairs + [copy for step in low_copies for copy in step]:
        copy.wait_send()
    for copy in back:
        copy.wait()

    @pl.when(ph == 1)
    def _():
        for copy in skips:
            copy.wait_send()


def cells_first(field):
    return field[0].transpose(1, 2, 0, 3)


def finish(gin_hbm, gq_hbm, gin_out, gq_out, gin_ref, gq_ref, in_sems, out_sems):
    halves = []
    for src, mid, dst in ((gin_hbm, gin_ref, gin_out), (gq_hbm, gq_ref, gq_out)):
        size = src.shape[0] // 2
        for k in range(2):
            at = pl.ds(size * k, size)
            n = len(halves)
            halves.append((
                pltpu.make_async_copy(src.at[at], mid.at[at], in_sems.at[n]),
                pltpu.make_async_copy(mid.at[at], dst.at[at], out_sems.at[n])))
    for load, _ in halves:
        load.start()
    for load, store in halves:
        load.wait()
        store.start()
    for _, store in halves:
        store.wait()


def per_device(n_lat, n_lon, x_in, out_grad, w_qkv, w_proj, norm_gain, bias_table, lat_labels):
    features = x_in.shape[-1]
    outs = w_qkv.shape[1]
    cols, rows = outs // n_lat, features // n_lon
    chunk = 128 if cols % 128 == 0 else cols
    chunks, half = cols // chunk, n_lon // 2
    vmem = pl.BlockSpec(memory_space=pltpu.VMEM)
    dma = lambda *shape: pltpu.SemaphoreType.DMA(shape)
    peers = max(n_lat - 1, 1)
    grid = (LAT, LON, LEV, features)
    grad_input, grad_qkv = pl.pallas_call(
        functools.partial(kernel, n_lat, n_lon, chunk),
        out_shape=(
            jax.ShapeDtypeStruct(grid, BF),
            jax.ShapeDtypeStruct((rows, cols), F32),
        ),
        in_specs=[pl.BlockSpec(memory_space=pl.ANY)] * 8,
        out_specs=(vmem, vmem),
        scratch_shapes=[
            pltpu.VMEM(grid, BF),
            pltpu.VMEM(grid, BF),
            pltpu.VMEM((outs, features), BF),
            pltpu.VMEM((features, features), BF),
            pltpu.VMEM((1, features), F32),
            pltpu.VMEM(bias_table.shape[1:], F32),
            pltpu.SMEM((LAT,), jnp.int32),
            pltpu.VMEM((WROWS + 256, 256), F32),
            pltpu.VMEM((8, 128), F32),
            pltpu.VMEM((8, 128), F32),
            pltpu.VMEM((8 * CELLS, 128), F32),
            pltpu.VMEM((8 * CELLS, 128), F32),
            pltpu.VMEM((HEADS // 2, 2 * ROWS, 128), F32),
            pltpu.VMEM((WROWS, outs), BF),
            pltpu.VMEM((HEADS, 2 * ROWS, ROWS), F32),
            pltpu.VMEM((WROWS, outs), F32),
            pltpu.VMEM((LEV, ROWS, features), BF),
            pltpu.VMEM((LEV, ROWS, features), BF),
            pltpu.VMEM(grid, BF),
            pltpu.VMEM((WROWS, features), BF),
            pltpu.VMEM((peers, WROWS, features), BF),
            pltpu.VMEM((n_lat, features, WROWS), BF),
            pltpu.VMEM((n_lat, chunks, WROWS, chunk), BF),
            pltpu.VMEM((peers, chunks, WROWS, chunk), BF),
            pltpu.VMEM((chunks, 2, half, rows, chunk), BF),
            pltpu.VMEM((chunks, half, rows, chunk), BF),
            pltpu.VMEM((chunks, half, rows, chunk), BF),
            pltpu.VMEM((chunks, half - 1, rows, chunk), BF),
            dma(8), dma(6), dma(6), dma(1), dma(1), dma(LEV), dma(LEV), dma(3), dma(3),
            dma(peers), dma(peers), dma(peers, chunks), dma(peers, chunks),
            dma(chunks), dma(chunks), dma(chunks, half - 1), dma(chunks, half - 1),
        ],
        compiler_params=pltpu.CompilerParams(
            collective_id=0, has_side_effects=True, vmem_limit_bytes=60 * 1024 * 1024),
    )(
        cells_first(x_in), cells_first(out_grad), w_qkv[0], w_proj[0], norm_gain,
        bias_table[0], lat_labels, jnp.asarray(selections()))
    grad_input, grad_qkv = pl.pallas_call(
        finish,
        out_shape=(
            jax.ShapeDtypeStruct(grid, BF),
            jax.ShapeDtypeStruct((rows, cols), F32),
        ),
        in_specs=[pl.BlockSpec(memory_space=pl.ANY)] * 2,
        out_specs=[pl.BlockSpec(memory_space=pl.ANY)] * 2,
        scratch_shapes=[
            pltpu.VMEM(grid, BF), pltpu.VMEM((rows, cols), F32), dma(4), dma(4)],
    )(grad_input, grad_qkv)
    return grad_input.transpose(2, 0, 1, 3)[None], grad_qkv.T[None]


def solution(mesh):
    in_specs = (
        P("phase", None, "lat", "lon", None),
        P("phase", None, "lat", "lon", None),
        P("phase", None, None),
        P("phase", None, None),
        P("phase", None),
        P("phase", None, None),
        P("lat"),
    )
    out_specs = (P("phase", None, "lat", "lon", None), P("phase", "lat", "lon"))
    return jax.shard_map(
        functools.partial(per_device, mesh.shape["lat"], mesh.shape["lon"]),
        mesh=mesh, in_specs=in_specs, out_specs=out_specs, check_vma=False)
```

```python
import functools

import jax
import jax.numpy as jnp
import numpy as np
from jax import lax
from jax.experimental import pallas as pl
from jax.experimental.pallas import tpu as pltpu
from jax.sharding import PartitionSpec as P

HEADS = 8
EPSILON = 1e-05
MASKED = -1e30
MESH = pl.DeviceIdType.MESH
BF = jnp.bfloat16
F32 = jnp.float32

LEV, LAT, LON = 2, 6, 12
CELLS = LAT * LON
ROWS = 80
WROWS = LEV * ROWS


def selections():
    packed = np.zeros((WROWS + 256, 256), np.float32)
    for n in range(CELLS):
        i, j = divmod(n, LON)
        for p in range(LEV):
            packed[ROWS * (1 - p) + n, LEV * n + p] = 1
        packed[WROWS + 126 - (23 * i + j), n] = 1
        packed[WROWS + 128 + (i + 3) % 6, n] = 1
    return packed


def dot(a, b, dims=((1,), (0,))):
    return lax.dot_general(a, b, (dims, ((), ())), preferred_element_type=F32)


NT = ((1,), (1,))
TN = ((0,), (0,))


def kernel(
    n_lat, n_lon, chunk,
    x_hbm, og_hbm, wqkv_hbm, wproj_hbm, gain_hbm, table_hbm, labels_hbm, select_hbm,
    gin_ref, gq_hbm,
    win_x, win_og, wqkv_ref, wproj_ref, gain_ref, table_ref, labels_ref, select_ref,
    send_lab, recv_lab, rolled, expanded, bias, proj, att, dqkv, cot, skip, back_src, gq_ref,
    scaled, scaled_in, turned, low, low_in, part, part_in, summed, summed_in,
    local_s, halo_s, halo_r, lab_s, lab_r, skip_s, skip_r, back_s, back_r,
    sc_s, sc_r, low_s, low_r, pair_s, pair_r, grp_s, grp_r,
):
    ph, la, lo = lax.axis_index("phase"), lax.axis_index("lat"), lax.axis_index("lon")
    features = gain_ref.shape[-1]
    rows, cols = gq_hbm.shape
    half = n_lon // 2
    chunks = cols // chunk
    par = lax.rem(lo, 2)
    grp = lo // 2

    def device(dlat, dlon):
        return (ph, lax.rem(la + dlat + n_lat, n_lat), lax.rem(lo + dlon + n_lon, n_lon))

    offsets = set()
    for dlat, dlon in ((0, 1), (1, 0), (1, 1)):
        offsets |= {(dlat % n_lat, dlon % n_lon), (-dlat % n_lat, -dlon % n_lon)}
    offsets |= {(d, 0) for d in range(1, n_lat)}
    offsets |= {(0, 2 * d) for d in range(1, half)}
    offsets = sorted(offsets)
    barrier = pltpu.get_barrier_semaphore()
    for dlat, dlon in offsets:
        pl.semaphore_signal(barrier, inc=1, device_id=device(dlat, dlon), device_id_type=MESH)
    pl.semaphore_signal(barrier, inc=1, device_id=(1 - ph, la, lo), device_id_type=MESH)

    def quadrant(ref, ih, jh):
        return ref.at[pl.ds(ih * LAT // 2, LAT // 2), pl.ds(jh * LON // 2, LON // 2)]

    loads = []
    for k, (src, dst) in enumerate((
        (labels_hbm, labels_ref),
        (table_hbm, table_ref),
        (select_hbm, select_ref),
        (quadrant(x_hbm, 1, 1), quadrant(win_x, 0, 0)),
        (gain_hbm, gain_ref),
        (wqkv_hbm, wqkv_ref),
        (quadrant(og_hbm, 1, 1), quadrant(win_og, 0, 0)),
        (wproj_hbm, wproj_ref),
    )):
        loads.append(pltpu.make_async_copy(src, dst, local_s.at[k]))
        loads[-1].start()
    pl.semaphore_wait(barrier, len(offsets) + 1)

    halo = []
    for src, dst in ((x_hbm, win_x), (og_hbm, win_og)):
        for ih, jh in ((0, 0), (1, 0), (0, 1)):
            k = len(halo)
            halo.append(pltpu.make_async_remote_copy(
                quadrant(src, ih, jh), quadrant(dst, 1 - ih, 1 - jh), halo_s.at[k], halo_r.at[k],
                device_id=device(ih - 1, jh - 1), device_id_type=MESH))
            halo[-1].start()
    loads[0].wait()
    lane = lax.broadcasted_iota(jnp.int32, (8, 128), 1)
    own_lab = jnp.zeros((8, 128), F32)
    for i in range(LAT):
        own_lab = jnp.where(lane == i, labels_ref[i].astype(F32), own_lab)
    send_lab[...] = own_lab

    lab_copy = pltpu.make_async_remote_copy(
        send_lab, recv_lab, lab_s.at[0], lab_r.at[0],
        device_id=device(-1, 0), device_id_type=MESH)
    lab_copy.start()
    for copy in loads[1:3]:
        copy.wait()

    table = table_ref[:, 128:512]
    for m in range(CELLS):
        i, j = divmod(m, LON)
        shift = (384 - (125 + 23 * i + j)) % 384
        rolled[8 * m:8 * m + 8, :] = pltpu.roll(table, shift, 1)[:, :128]
    wide = rolled[...]
    high = wide.astype(BF)
    rest = wide - high.astype(F32)
    mid = rest.astype(BF)
    least = (rest - mid.astype(F32)).astype(BF)
    column = select_ref[WROWS:WROWS + 128, :128].astype(BF)
    expanded[...] = (dot(high, column) + dot(mid, column)) + dot(least, column)

    lab_copy.wait()
    lab = jnp.where(lane < 3, recv_lab[...], own_lab)
    lab_row = dot(jnp.concatenate([lab, lab], axis=0).astype(BF), select_ref[WROWS + 128:WROWS + 256, :128].astype(BF))[0:1]
    lane1 = lax.broadcasted_iota(jnp.int32, (1, 128), 1)
    lab_row = jnp.where(lane1 < CELLS, lab_row, -1.0)
    row_id = lax.broadcasted_iota(jnp.int32, (ROWS, 128), 0)
    lane_id = lax.broadcasted_iota(jnp.int32, (ROWS, 128), 1)
    want = jnp.zeros((ROWS, 128), jnp.int32)
    for i in range(LAT):
        want = jnp.where(row_id >= LON * i, (i + 3) % 6, want)
    lab_col = jnp.sum(jnp.where(lane_id == want, lab[0:1], 0.0), axis=1, keepdims=True)
    row1 = lax.broadcasted_iota(jnp.int32, (ROWS, 1), 0)
    lab_col = jnp.where(row1 < CELLS, lab_col, -1.0)
    allowed = lab_col == lab_row
    for h in range(HEADS):
        one = expanded[pl.ds(h, CELLS, stride=8), :]
        one = jnp.concatenate([one, jnp.zeros((ROWS - CELLS, 128), F32)], axis=0)
        bias[h // 2, ROWS * (h % 2):ROWS * (h % 2 + 1), :] = jnp.where(allowed, one, MASKED)

    for copy in loads[3:6] + halo[:3]:
        copy.wait()
    to_win = select_ref[:WROWS, :LEV * CELLS].astype(BF)
    x = dot(to_win, win_x[...].reshape(LEV * CELLS, features))
    gain = gain_ref[...]
    center = jnp.mean(x, axis=-1, keepdims=True)
    spread = jnp.mean(jnp.square(x - center), axis=-1, keepdims=True)
    inv_std = lax.rsqrt(spread + EPSILON)
    normed = (x - center) * inv_std
    scaled[...] = (normed * gain).astype(BF)
    sc_copies = []
    for d in range(1, n_lat):
        sc_copies.append(pltpu.make_async_remote_copy(
            scaled, scaled_in.at[d - 1], sc_s.at[d - 1], sc_r.at[d - 1],
            device_id=device(d, 0), device_id_type=MESH))
        sc_copies[-1].start()
    proj[...] = dot(scaled[...], wqkv_ref[...], NT).astype(BF)
    first_half = lax.broadcasted_iota(jnp.int32, (ROWS, 128), 1) < 64
    zero = jnp.zeros((ROWS, 128), BF)

    def both(pair):
        return jnp.concatenate(
            [jnp.where(first_half, pair, zero), jnp.where(first_half, zero, pair)], axis=0)

    def query_pair(p, hp):
        pair = proj[ROWS * p:ROWS * (p + 1), 128 * hp:128 * (hp + 1)]
        return both(pair * jnp.asarray(0.125, BF))

    def later_pair(which, p, hp):
        start = features * which + 128 * hp
        return proj[ROWS * p:ROWS * (p + 1), start:start + 128]

    pairs_of = range(HEADS // 2)
    units = [(p, hp) for p in range(LEV) for hp in pairs_of]
    scores = [
        dot(query_pair(p, hp), later_pair(1, p, hp), NT) + bias[hp][:, :ROWS] for p, hp in units]
    weights = [jnp.exp(s - jnp.max(s, axis=-1, keepdims=True)) for s in scores]
    scales = [1.0 / jnp.sum(w, axis=-1, keepdims=True) for w in weights]
    for k, (w, scale) in enumerate(zip(weights, scales)):
        att[k] = w * scale

    def attended_grad(p, cotangent):
        return dot(cotangent, wproj_ref[...]).astype(BF)

    def attention_grad(p, d_attended, accumulate):
        d_pairs = [both(d_attended[:, 128 * hp:128 * (hp + 1)]) for hp in pairs_of]
        d_probs = [dot(d_pairs[hp], later_pair(2, p, hp), NT) for hp in pairs_of]
        d_values = [dot(att[4 * p + hp].astype(BF), d_pairs[hp], TN) for hp in pairs_of]
        inner = [
            jnp.sum(att[4 * p + hp] * d_probs[hp], axis=-1, keepdims=True) for hp in pairs_of]
        d_scores = [
            (att[4 * p + hp] * (d_probs[hp] - inner[hp])).astype(BF) for hp in pairs_of]
        d_both = [dot(d_scores[hp], later_pair(1, p, hp)) for hp in pairs_of]
        d_keys = [dot(d_scores[hp], query_pair(p, hp), TN) for hp in pairs_of]
        d_queries = [jnp.where(first_half, d[:ROWS], d[ROWS:]) * 0.125 for d in d_both]
        values = d_queries + d_keys + d_values
        for k, value in enumerate(values):
            at = (slice(ROWS * p, ROWS * (p + 1)), slice(128 * k, 128 * (k + 1)))
            dqkv[at] = dqkv[at] + value if accumulate else value
        return [value.astype(BF) for value in values]

    def input_grad(p, lows):
        own = slice(ROWS * p, ROWS * (p + 1))
        d_normed = dot(jnp.concatenate(lows, axis=1), wqkv_ref[...]) * gain
        return inv_std[own] * (
            d_normed
            - jnp.mean(d_normed, axis=-1, keepdims=True)
            - normed[own] * jnp.mean(d_normed * normed[own], axis=-1, keepdims=True))

    for copy in loads[6:] + halo[3:]:
        copy.wait()
    og = dot(to_win, win_og[...].reshape(LEV * CELLS, features))
    totals, skips = [], []
    for p in range(LEV):
        og_p = og[ROWS * p:ROWS * (p + 1)]
        d_attended = attended_grad(p, og_p.astype(BF))
        totals.append(og_p + input_grad(p, attention_grad(p, d_attended, False)))
        cot[p] = totals[p].astype(BF)
        skips.append(pltpu.make_async_remote_copy(
            cot.at[p], skip.at[p], skip_s.at[p], skip_r.at[p],
            device_id=(1 - ph, la, lo), device_id_type=MESH))
        pl.when(ph == 1)(skips[p].start)

    turned[0] = scaled[...].T
    for d in range(1, n_lat):
        sc_copies[d - 1].wait()
        turned[d] = scaled_in[d - 1].T
    low_copies, pairs = [], []
    for c in range(chunks):
        low_copies.append([])
        for d in range(1, n_lat):
            to = device(d, 0)
            low_copies[c].append(pltpu.make_async_remote_copy(
                low.at[to[1], c], low_in.at[d - 1, c], low_s.at[d - 1, c], low_r.at[d - 1, c],
                device_id=to, device_id_type=MESH))
        pairs.append(pltpu.make_async_remote_copy(
            part.at[c, 1 - par], part_in.at[c], pair_s.at[c], pair_r.at[c],
            device_id=(ph, la, lo + 1 - 2 * par), device_id_type=MESH))

    def send_factors(c):
        for l in range(n_lat):
            start = cols * l + chunk * c
            low[l, c] = dqkv[:, start:start + chunk].astype(BF)
        for copy in low_copies[c]:
            copy.start()

    def send_sums(c):
        for copy in low_copies[c]:
            copy.wait_recv()
        value = dot(turned[0], low[la, c])
        for d in range(1, n_lat):
            value = value + dot(turned[d], low_in[d - 1, c])
        value = value.astype(BF)
        for j in range(n_lon):
            part[c, j % 2, j // 2] = value[rows * j:rows * (j + 1)]
        pairs[c].start()

    @pl.when(ph == 1)
    def _():
        for c in range(chunks):
            send_factors(c)
        for c in range(chunks):
            send_sums(c)

    @pl.when(ph == 0)
    def _():
        skips[0].wait_recv()
        d_attended = attended_grad(0, skip[0])
        lows = attention_grad(0, d_attended, True)
        cot[0] = (totals[0] + (skip[0].astype(F32) + input_grad(0, lows))).astype(BF)
        skips[1].wait_recv()
        d_attended = attended_grad(1, skip[1])
        lows = attention_grad(1, d_attended, True)
        for c in range(chunks):
            send_factors(c)
        cot[1] = (totals[1] + (skip[1].astype(F32) + input_grad(1, lows))).astype(BF)
        for c in range(chunks):
            send_sums(c)

    whole = cot[...].reshape(WROWS, features)
    back_src[...] = dot(to_win, whole, TN).astype(BF).reshape(LAT, LON, LEV, features)
    back = []
    for ih, jh in ((0, 0), (0, 1), (1, 0)):
        k = len(back)
        back.append(pltpu.make_async_remote_copy(
            quadrant(back_src, 1 - ih, 1 - jh), quadrant(gin_ref, ih, jh), back_s.at[k], back_r.at[k],
            device_id=device(1 - ih, 1 - jh), device_id_type=MESH))
    results = [pltpu.make_async_copy(
        quadrant(back_src, 0, 0), quadrant(gin_ref, 1, 1), local_s.at[0])]
    results[0].start()

    for copy in back:
        copy.start()
    groups = []
    for c in range(chunks):
        pairs[c].wait_recv()
        summed[c] = (part[c, par].astype(F32) + part_in[c].astype(F32)).astype(BF)
        for d in range(1, half):
            to = lax.rem(grp + d, half)
            groups.append(pltpu.make_async_remote_copy(
                summed.at[c, to], summed_in.at[c, d - 1],
                grp_s.at[c, d - 1], grp_r.at[c, d - 1],
                device_id=(ph, la, 2 * to + par), device_id_type=MESH))
            groups[-1].start()

    for c in range(chunks):
        value = summed[c, grp].astype(F32)
        for d in range(1, half):
            groups[c * (half - 1) + d - 1].wait_recv()
            value = value + summed_in[c, d - 1].astype(F32)
        at = pl.ds(chunk * c, chunk)
        gq_ref[:, at] = value
        results.append(pltpu.make_async_copy(gq_ref.at[:, at], gq_hbm.at[:, at], local_s.at[c + 1]))
        results[-1].start()

    for copy in groups:
        copy.wait_send()
    for copy in pairs + [copy for step in low_copies for copy in step]:
        copy.wait_send()
    for copy in back + results:
        copy.wait()

    @pl.when(ph == 1)
    def _():
        for copy in skips:
            copy.wait_send()


def cells_first(field):
    return field[0].transpose(1, 2, 0, 3)


def finish(gin_hbm, gq_hbm, gin_out, gq_out, gin_ref, gq_ref, in_sems, out_sems):
    halves = []
    for src, mid, dst in ((gin_hbm, gin_ref, gin_out), (gq_hbm, gq_ref, gq_out)):
        size = src.shape[0] // 2
        for k in range(2):
            at = pl.ds(size * k, size)
            n = len(halves)
            halves.append((
                pltpu.make_async_copy(src.at[at], mid.at[at], in_sems.at[n]),
                pltpu.make_async_copy(mid.at[at], dst.at[at], out_sems.at[n])))
    for load, _ in halves:
        load.start()
    for load, store in halves:
        load.wait()
        store.start()
    for _, store in halves:
        store.wait()


def per_device(n_lat, n_lon, x_in, out_grad, w_qkv, w_proj, norm_gain, bias_table, lat_labels):
    features = x_in.shape[-1]
    outs = w_qkv.shape[1]
    cols, rows = outs // n_lat, features // n_lon
    chunk = 128 if cols % 128 == 0 else cols
    chunks, half = cols // chunk, n_lon // 2
    dma = lambda *shape: pltpu.SemaphoreType.DMA(shape)
    peers = max(n_lat - 1, 1)
    grid = (LAT, LON, LEV, features)
    grad_input, grad_qkv = pl.pallas_call(
        functools.partial(kernel, n_lat, n_lon, chunk),
        out_shape=(
            jax.ShapeDtypeStruct(grid, BF),
            jax.ShapeDtypeStruct((rows, cols), F32),
        ),
        in_specs=[pl.BlockSpec(memory_space=pl.ANY)] * 8,
        out_specs=[pl.BlockSpec(memory_space=pl.ANY)] * 2,
        scratch_shapes=[
            pltpu.VMEM(grid, BF),
            pltpu.VMEM(grid, BF),
            pltpu.VMEM((outs, features), BF),
            pltpu.VMEM((features, features), BF),
            pltpu.VMEM((1, features), F32),
            pltpu.VMEM(bias_table.shape[1:], F32),
            pltpu.SMEM((LAT,), jnp.int32),
            pltpu.VMEM((WROWS + 256, 256), F32),
            pltpu.VMEM((8, 128), F32),
            pltpu.VMEM((8, 128), F32),
            pltpu.VMEM((8 * CELLS, 128), F32),
            pltpu.VMEM((8 * CELLS, 128), F32),
            pltpu.VMEM((HEADS // 2, 2 * ROWS, 128), F32),
            pltpu.VMEM((WROWS, outs), BF),
            pltpu.VMEM((HEADS, 2 * ROWS, ROWS), F32),
            pltpu.VMEM((WROWS, outs), F32),
            pltpu.VMEM((LEV, ROWS, features), BF),
            pltpu.VMEM((LEV, ROWS, features), BF),
            pltpu.VMEM(grid, BF),
            pltpu.VMEM((rows, cols), F32),
            pltpu.VMEM((WROWS, features), BF),
            pltpu.VMEM((peers, WROWS, features), BF),
            pltpu.VMEM((n_lat, features, WROWS), BF),
            pltpu.VMEM((n_lat, chunks, WROWS, chunk), BF),
            pltpu.VMEM((peers, chunks, WROWS, chunk), BF),
            pltpu.VMEM((chunks, 2, half, rows, chunk), BF),
            pltpu.VMEM((chunks, half, rows, chunk), BF),
            pltpu.VMEM((chunks, half, rows, chunk), BF),
            pltpu.VMEM((chunks, half - 1, rows, chunk), BF),
            dma(max(8, chunks + 1)), dma(6), dma(6), dma(1), dma(1), dma(LEV), dma(LEV), dma(3), dma(3),
            dma(peers), dma(peers), dma(peers, chunks), dma(peers, chunks),
            dma(chunks), dma(chunks), dma(chunks, half - 1), dma(chunks, half - 1),
        ],
        compiler_params=pltpu.CompilerParams(
            collective_id=0, has_side_effects=True, vmem_limit_bytes=60 * 1024 * 1024),
    )(
        cells_first(x_in), cells_first(out_grad), w_qkv[0], w_proj[0], norm_gain,
        bias_table[0], lat_labels, jnp.asarray(selections()))
    grad_input, grad_qkv = pl.pallas_call(
        finish,
        out_shape=(
            jax.ShapeDtypeStruct(grid, BF),
            jax.ShapeDtypeStruct((rows, cols), F32),
        ),
        in_specs=[pl.BlockSpec(memory_space=pl.ANY)] * 2,
        out_specs=[pl.BlockSpec(memory_space=pl.ANY)] * 2,
        scratch_shapes=[
            pltpu.VMEM(grid, BF), pltpu.VMEM((rows, cols), F32), dma(4), dma(4)],
    )(grad_input, grad_qkv)
    return grad_input.transpose(2, 0, 1, 3)[None], grad_qkv.T[None]


def solution(mesh):
    in_specs = (
        P("phase", None, "lat", "lon", None),
        P("phase", None, "lat", "lon", None),
        P("phase", None, None),
        P("phase", None, None),
        P("phase", None),
        P("phase", None, None),
        P("lat"),
    )
    out_specs = (P("phase", None, "lat", "lon", None), P("phase", "lat", "lon"))
    return jax.shard_map(
        functools.partial(per_device, mesh.shape["lat"], mesh.shape["lon"]),
        mesh=mesh, in_specs=in_specs, out_specs=out_specs, check_vma=False)
```
